32 devices in a mesh: dp: 8 (over y, x, core), own: 4 (over z).
Axes of the slice: x: 2, y: 2, z: 4, core: 2. Of those that a mesh axis runs over, the one named last changes fastest.
Arguments:
- hidden: bfloat16 [8192, 2560], P(('dp', 'own')), may hold values from -6 to 6
- cotangent: bfloat16 [8192, 2560], P(('dp', 'own')), may hold values from -6 to 6
- block_index: int32 [8, 1024], P('dp'), may hold values from 0 to 5, never falling along the last dimension, each value on 1 to 256 neighbouring positions
- owners: int32 [9], replicated, may hold values from 0 to 3
- query_down: float32 [4, 2560, 768], P('own', 'dp'), may hold values from -0.125 to 0.125
- query_down_first: float32 [4, 2560, 768], P('own', 'dp'), may hold values from -1792 to 1792
- query_down_second: float32 [4, 2560, 768], P('own', 'dp'), may hold values from 81920 to 327680
- query_up: float32 [4, 768, 3840], P('own', 'dp'), may hold values from -0.21875 to 0.21875
- query_up_first: float32 [4, 768, 3840], P('own', 'dp'), may hold values from -896 to 896
- query_up_second: float32 [4, 768, 3840], P('own', 'dp'), may hold values from 21299.2 to 81920
- latent_down: float32 [4, 2560, 288], P('own', 'dp'), may hold values from -0.125 to 0.125
- latent_down_first: float32 [4, 2560, 288], P('own', 'dp'), may hold values from -3584 to 3584
- latent_down_second: float32 [4, 2560, 288], P('own', 'dp'), may hold values from 327680 to 1310720
- latent_up: float32 [4, 256, 5120], P('own', 'dp'), may hold values from -0.375 to 0.375
- latent_up_first: float32 [4, 256, 5120], P('own', 'dp'), may hold values from -896 to 896
- latent_up_second: float32 [4, 256, 5120], P('own', 'dp'), may hold values from 21299.2 to 81920
- output_weight: float32 [4, 2560, 2560], P('own', 'dp'), may hold values from -15.094638 to 15.094638
- output_weight_first: float32 [4, 2560, 2560], P('own', 'dp'), may hold values from -7 to 7
- output_weight_second: float32 [4, 2560, 2560], P('own', 'dp'), may hold values from 1.28 to 5.12
- gate_weight: float32 [4, 2560, 6400], P('own', 'dp'), may hold values from -0.125 to 0.125
- gate_weight_first: float32 [4, 2560, 6400], P('own', 'dp'), may hold values from -512 to 512
- gate_weight_second: float32 [4, 2560, 6400], P('own', 'dp'), may hold values from 5734.4 to 22937.6
- up_weight: float32 [4, 2560, 6400], P('own', 'dp'), may hold values from -0.125 to 0.125
- up_weight_first: float32 [4, 2560, 6400], P('own', 'dp'), may hold values from -512 to 512
- up_weight_second: float32 [4, 2560, 6400], P('own', 'dp'), may hold values from 6553.6 to 26214.4
- down_weight: float32 [4, 6400, 2560], P('own', 'dp'), may hold values from -0.70243937 to 0.70243937
- down_weight_first: float32 [4, 6400, 2560], P('own', 'dp'), may hold values from -56 to 56
- down_weight_second: float32 [4, 6400, 2560], P('own', 'dp'), may hold values from 81.92 to 327.68
- norm_gains: float32 [4, 6144], P('own', 'dp'), may hold values from 0.5 to 1.5
- norm_gains_first: float32 [4, 6144], P('own', 'dp'), may hold values from -2048 to 2048
- norm_gains_second: float32 [4, 6144], P('own', 'dp'), may hold values from 131072 to 524288
Outputs:
- block_output: bfloat16 [8192, 2560], P(('dp', 'own'))
- input_grad: bfloat16 [8192, 2560], P(('dp', 'own'))
- new_query_down: float32 [4, 2560, 768], P('own', 'dp')
- new_query_down_first: float32 [4, 2560, 768], P('own', 'dp')
- new_query_down_second: float32 [4, 2560, 768], P('own', 'dp')
- new_query_up: float32 [4, 768, 3840], P('own', 'dp')
- new_query_up_first: float32 [4, 768, 3840], P('own', 'dp')
- new_query_up_second: float32 [4, 768, 3840], P('own', 'dp')
- new_latent_down: float32 [4, 2560, 288], P('own', 'dp')
- new_latent_down_first: float32 [4, 2560, 288], P('own', 'dp')
- new_latent_down_second: float32 [4, 2560, 288], P('own', 'dp')
- new_latent_up: float32 [4, 256, 5120], P('own', 'dp')
- new_latent_up_first: float32 [4, 256, 5120], P('own', 'dp')
- new_latent_up_second: float32 [4, 256, 5120], P('own', 'dp')
- new_output_weight: float32 [4, 2560, 2560], P('own', 'dp')
- new_output_weight_first: float32 [4, 2560, 2560], P('own', 'dp')
- new_output_weight_second: float32 [4, 2560, 2560], P('own', 'dp')
- new_gate_weight: float32 [4, 2560, 6400], P('own', 'dp')
- new_gate_weight_first: float32 [4, 2560, 6400], P('own', 'dp')
- new_gate_weight_second: float32 [4, 2560, 6400], P('own', 'dp')
- new_up_weight: float32 [4, 2560, 6400], P('own', 'dp')
- new_up_weight_first: float32 [4, 2560, 6400], P('own', 'dp')
- new_up_weight_second: float32 [4, 2560, 6400], P('own', 'dp')
- new_down_weight: float32 [4, 6400, 2560], P('own', 'dp')
- new_down_weight_first: float32 [4, 6400, 2560], P('own', 'dp')
- new_down_weight_second: float32 [4, 6400, 2560], P('own', 'dp')
- new_norm_gains: float32 [4, 6144], P('own', 'dp')
- new_norm_gains_first: float32 [4, 6144], P('own', 'dp')
- new_norm_gains_second: float32 [4, 6144], P('own', 'dp')
The draws below stay inside these ranges and needn't reach their ends.
Inputs may be any that keep to these rules, and one draw needn't show every extreme that they name: `block_index`: along each sequence the block numbers never fall; each block holds 1 to 256 positions and one holds exactly 256.
All inputs are finite; a program needn't handle non-finite values.
Results may differ from the reference program's by a relative error of at most 0.022.
Values may be sent and summed in bfloat16 or wider, within the bound.
No kernel may reach another device: no remote copies, remote signals or barrier semaphores. Data moves between devices by JAX's collectives and lax.ppermute only.
A program may use at most 576 MiB of HBM per device.

```python
import math
import jax
import jax.numpy as jnp
import numpy as np
from jax import lax

D = 2560
H = 40
NOPE = 64
ROPE = 32
VD = 64
QR = 768
KVR = 256
FF = 6400
BLOCK = 256
STEP = 7
LENGTH = 1024
SEQS = 8
TOKENS = 8192
GAINS = 6144
N_OWN = 4


def plant(array, own_key, smallest, largest):
    extent = array.shape
    place = [jax.random.randint(jax.random.fold_in(own_key, axis), (), 0, extent[axis]) for axis in range(len(extent))]
    array = array.at[tuple(place)].set(smallest)
    longest = extent.index(max(extent))
    place[longest] = (place[longest] + 1) % extent[longest]
    return array.at[tuple(place)].set(largest)


def level_of(own_key, shape, cuts, low, high):
    gain = 1.0
    for dim, shards_of in cuts:
        steps = jax.random.uniform(jax.random.fold_in(jax.random.fold_in(own_key, 6), dim), (shards_of,), jnp.float32, low / len(cuts), high / len(cuts))
        gain = gain * jnp.repeat(jnp.exp(steps), shape[dim] // shards_of).reshape((-1,) + (1,) * (len(shape) - 1 - dim))
    return gain


def length_profile(count, total, limit, slope):
    loads = [(1 << 20) // math.isqrt(grade ** slope) + 1 for grade in range(2, count + 1)]
    spare, given = total - limit - (count - 1), [1] * (count - 1)
    while spare > 0:
        free = [i for i in range(count - 1) if given[i] < limit]
        pool, left = sum([loads[i] for i in free]), spare
        for i in free:
            addition = min(limit - given[i], max(1, left * loads[i] // pool), spare)
            given[i] = given[i] + addition
            spare = spare - addition
    return np.array([limit] + given)


def uneven_parts(key, count, total, bound, slope):
    if count == 2:
        one = jax.random.randint(key, (), max(1, total - bound), min(bound, total - 1) + 1)
        return jnp.stack([one, total - one])
    tallies = jnp.asarray(length_profile(count, total, bound, slope), jnp.int32)
    pairs = (count - 1) // 2
    donor, sink = tallies[1:1 + 2 * pairs:2], tallies[2:2 + 2 * pairs:2]
    margin = jnp.minimum(donor - 1, bound - sink)
    passed = jax.random.randint(jax.random.fold_in(key, 1), (pairs,), 0, 1 << 20) % (margin + 1)
    tallies = tallies.at[1:1 + 2 * pairs:2].set(donor - passed).at[2:2 + 2 * pairs:2].set(sink + passed)
    return tallies[jax.random.permutation(jax.random.fold_in(key, 2), count)]


def centred(own_key, shape, scale, most, cuts=(), kind=jnp.bfloat16):
    array = jax.random.normal(own_key, shape, jnp.float32) * scale
    if len(cuts) > 0:
        array = level_of(own_key, shape, cuts, -0.22, 0.18) * array
    return jnp.clip(array, min=-most, max=most).astype(kind)


def setup_inputs(seed: int = 0) -> dict:
    arg_keys = jax.random.split(jax.random.key(seed), 32)
    hidden = centred(arg_keys[0], (TOKENS, D), 1.0, 6.0, ((0, 32),))
    cotangent = centred(arg_keys[1], (TOKENS, D), 1.0, 6.0, ((0, 32),))
    block_index = jax.vmap(lambda own: jnp.searchsorted(jnp.cumsum(uneven_parts(own, 3 * LENGTH // (2 * BLOCK), LENGTH, BLOCK, 0)), jnp.arange(LENGTH), side="right"))(jax.random.split(arg_keys[2], SEQS)).reshape((SEQS, LENGTH)).astype(jnp.int32)
    owners = plant(jax.random.randint(arg_keys[3], (9,), 0, N_OWN), jax.random.fold_in(arg_keys[3], 1), 0, N_OWN - 1).astype(jnp.int32)
    query_down = centred(arg_keys[4], (N_OWN, D, QR), D ** -0.5, 0.125, ((0, 4), (1, 8)), jnp.float32)
    query_down_first = centred(arg_keys[5], (N_OWN, D, QR), (3.2 * TOKENS ** 0.5), 1792.0, ((0, 4), (1, 8)), jnp.float32)
    query_down_second = jnp.clip(jnp.exp(math.log(327680.0) - 1.3862944 * jax.random.uniform(arg_keys[6], (N_OWN, D, QR), jnp.float32) ** level_of(arg_keys[6], (N_OWN, D, QR), ((0, 4), (1, 8)), -0.2, 0.2)), 81920.0, 327680.0)
    query_up = centred(arg_keys[7], (N_OWN, QR, H * (NOPE + ROPE)), QR ** -0.5, 0.21875, ((0, 4), (1, 8)), jnp.float32)
    query_up_first = centred(arg_keys[8], (N_OWN, QR, H * (NOPE + ROPE)), (1.6 * TOKENS ** 0.5), 896.0, ((0, 4), (1, 8)), jnp.float32)
    query_up_second = jnp.clip(jnp.exp(math.log(81920.0) - 1.3470737 * jax.random.uniform(arg_keys[9], (N_OWN, QR, H * (NOPE + ROPE)), jnp.float32) ** level_of(arg_keys[9], (N_OWN, QR, H * (NOPE + ROPE)), ((0, 4), (1, 8)), -0.2, 0.2)), 21299.2, 81920.0)
    latent_down = centred(arg_keys[10], (N_OWN, D, KVR + ROPE), D ** -0.5, 0.125, ((0, 4), (1, 8)), jnp.float32)
    latent_down_first = centred(arg_keys[11], (N_OWN, D, KVR + ROPE), (6.4 * TOKENS ** 0.5), 3584.0, ((0, 4), (1, 8)), jnp.float32)
    latent_down_second = jnp.clip(jnp.exp(math.log(1310720) - 1.3862944 * jax.random.uniform(arg_keys[12], (N_OWN, D, KVR + ROPE), jnp.float32) ** level_of(arg_keys[12], (N_OWN, D, KVR + ROPE), ((0, 4), (1, 8)), -0.2, 0.2)), 327680.0, 1310720)
    latent_up = centred(arg_keys[13], (N_OWN, KVR, H * (NOPE + VD)), KVR ** -0.5, 0.375, ((0, 4), (1, 8)), jnp.float32)
    latent_up_first = centred(arg_keys[14], (N_OWN, KVR, H * (NOPE + VD)), (1.6 * TOKENS ** 0.5), 896.0, ((0, 4), (1, 8)), jnp.float32)
    latent_up_second = jnp.clip(jnp.exp(math.log(81920.0) - 1.3470737 * jax.random.uniform(arg_keys[15], (N_OWN, KVR, H * (NOPE + VD)), jnp.float32) ** level_of(arg_keys[15], (N_OWN, KVR, H * (NOPE + VD)), ((0, 4), (1, 8)), -0.2, 0.2)), 21299.2, 81920.0)
    output_weight = centred(arg_keys[16], (N_OWN, H * VD, D), ((LENGTH / (0.0632 * H * VD)) ** 0.5), 15.094638, ((0, 4), (1, 8)), jnp.float32)
    output_weight_first = centred(arg_keys[17], (N_OWN, H * VD, D), (0.4 * (TOKENS / LENGTH) ** 0.5), 7.0, ((0, 4), (1, 8)), jnp.float32)
    output_weight_second = jnp.clip(jnp.exp(math.log(5.12) - 1.3862944 * jax.random.uniform(arg_keys[18], (N_OWN, H * VD, D), jnp.float32) ** level_of(arg_keys[18], (N_OWN, H * VD, D), ((0, 4), (1, 8)), -0.2, 0.2)), 1.28, 5.12)
    gate_weight = centred(arg_keys[19], (N_OWN, D, FF), D ** -0.5, 0.125, ((0, 4), (1, 8)), jnp.float32)
    gate_weight_first = centred(arg_keys[20], (N_OWN, D, FF), (0.9 * TOKENS ** 0.5), 512.0, ((0, 4), (1, 8)), jnp.float32)
    gate_weight_second = jnp.clip(jnp.exp(math.log(22937.6) - 1.3862944 * jax.random.uniform(arg_keys[21], (N_OWN, D, FF), jnp.float32) ** level_of(arg_keys[21], (N_OWN, D, FF), ((0, 4), (1, 8)), -0.2, 0.2)), 5734.4, 22937.6)
    up_weight = centred(arg_keys[22], (N_OWN, D, FF), D ** -0.5, 0.125, ((0, 4), (1, 8)), jnp.float32)
    up_weight_first = centred(arg_keys[23], (N_OWN, D, FF), (1.0 * TOKENS ** 0.5), 512.0, ((0, 4), (1, 8)), jnp.float32)
    up_weight_second = jnp.clip(jnp.exp(math.log(26214.4) - 1.3862944 * jax.random.uniform(arg_keys[24], (N_OWN, D, FF), jnp.float32) ** level_of(arg_keys[24], (N_OWN, D, FF), ((0, 4), (1, 8)), -0.2, 0.2)), 6553.6, 26214.4)
    down_weight = centred(arg_keys[25], (N_OWN, FF, D), ((1 / (0.0114 * FF)) ** 0.5), 0.70243937, ((0, 4), (1, 8)), jnp.float32)
    down_weight_first = centred(arg_keys[26], (N_OWN, FF, D), (0.1 * TOKENS ** 0.5), 56.0, ((0, 4), (1, 8)), jnp.float32)
    down_weight_second = jnp.clip(jnp.exp(math.log(327.68) - 1.3862944 * jax.random.uniform(arg_keys[27], (N_OWN, FF, D), jnp.float32) ** level_of(arg_keys[27], (N_OWN, FF, D), ((0, 4), (1, 8)), -0.2, 0.2)), 81.92, 327.68)
    norm_gains = jnp.clip(1.0 + 0.1 * jax.random.normal(arg_keys[28], (N_OWN, GAINS), jnp.float32), 0.5, 1.5)
    norm_gains_first = centred(arg_keys[29], (N_OWN, GAINS), (4 * TOKENS ** 0.5), 2048.0, ((0, 4), (1, 8)), jnp.float32)
    norm_gains_second = jnp.clip(jnp.exp(math.log(524288.0) - 1.3862944 * jax.random.uniform(arg_keys[30], (N_OWN, GAINS), jnp.float32) ** level_of(arg_keys[30], (N_OWN, GAINS), ((0, 4), (1, 8)), -0.2, 0.2)), 131072.0, 524288.0)
    return dict(hidden=hidden, cotangent=cotangent, block_index=block_index, owners=owners, query_down=query_down, query_down_first=query_down_first, query_down_second=query_down_second, query_up=query_up, query_up_first=query_up_first, query_up_second=query_up_second, latent_down=latent_down, latent_down_first=latent_down_first, latent_down_second=latent_down_second, latent_up=latent_up, latent_up_first=latent_up_first, latent_up_second=latent_up_second, output_weight=output_weight, output_weight_first=output_weight_first, output_weight_second=output_weight_second, gate_weight=gate_weight, gate_weight_first=gate_weight_first, gate_weight_second=gate_weight_second, up_weight=up_weight, up_weight_first=up_weight_first, up_weight_second=up_weight_second, down_weight=down_weight, down_weight_first=down_weight_first, down_weight_second=down_weight_second, norm_gains=norm_gains, norm_gains_first=norm_gains_first, norm_gains_second=norm_gains_second)


EPSILON = 1e-05
RESIDUAL_SCALE = 1.4 / math.sqrt(62.0)
BETA_ONE = 0.5
BETA_TWO = 0.55
WEIGHT_DECAY = 0.1
ADAM_EPS = 1e-08
HIGHEST = lax.Precision.HIGHEST

@jax.custom_vjp
def low(v):
    return lax.optimization_barrier(v.astype(jnp.bfloat16)).astype(jnp.float32)

@jax.custom_vjp
def low_back(v):
    return v

def low_keep(v):
    return (low(v), None)

def low_pass(kept, grad):
    return (grad,)

def back_keep(v):
    return (v, None)

def back_low(kept, grad):
    return (low(grad),)
low.defvjp(low_keep, low_pass)
low_back.defvjp(back_keep, back_low)

def rms_normed(values, norm_gain):
    return values * lax.rsqrt(lax.optimization_barrier(jnp.mean(values * values, axis=-1, keepdims=True)) + EPSILON) * norm_gain

def rotary_tables():
    half_width = ROPE // 2
    frequency = 10000.0 ** (-jnp.arange(half_width, dtype=jnp.float32) / half_width)
    angles = jnp.arange(LENGTH, dtype=jnp.float32)[:, None] * frequency[None, :]
    return (jnp.cos(angles), jnp.sin(angles))

def rotate(values, cosine, sine_table):
    half_width = values.shape[-1] // 2
    former = values[..., :half_width]
    latter = values[..., half_width:]
    return jnp.concatenate([former * cosine - latter * sine_table, latter * cosine + former * sine_table], axis=-1)

def attend_rows(query_rows, key_value, rope_keys, query_blocks, key_blocks):
    raw_scores = jnp.einsum('qhd,khd->hqk', query_rows[..., :NOPE], key_value[..., :NOPE], precision=HIGHEST)
    raw_scores = raw_scores + jnp.einsum('qhd,kd->hqk', query_rows[..., NOPE:], rope_keys, precision=HIGHEST)
    scores = low_back(raw_scores * (NOPE + ROPE) ** (-0.5))
    scores = jnp.where(key_blocks[None, None, :] <= query_blocks[None, :, None], scores, -1e+30)
    row_peak = lax.optimization_barrier(jnp.max(scores, axis=-1, keepdims=True))
    exponent = jnp.exp(scores - row_peak)
    weights_low = low(exponent / lax.optimization_barrier(jnp.sum(exponent, axis=-1, keepdims=True)))
    return jnp.einsum('hqk,khd->qhd', weights_low, key_value[..., NOPE:], precision=HIGHEST)

def sequence_forward(inputs, sequence_blocks, weights):
    query_down, query_up, latent_down, latent_up, output_weight, gate_weight, up_weight, down_weight, norm_gains = weights
    gain_input = norm_gains[:D]
    gain_query = norm_gains[D:D + QR]
    gain_latent = norm_gains[D + QR:D + QR + KVR]
    gain_ffn = norm_gains[D + QR + KVR:]
    normed = low(rms_normed(inputs, gain_input))
    query_latent = low_back(jnp.dot(normed, query_down, precision=HIGHEST))
    query_low = low(rms_normed(query_latent, gain_query))
    query_raw = low_back(jnp.dot(query_low, query_up, precision=HIGHEST)).reshape(LENGTH, H, NOPE + ROPE)
    cosine, sine_table = rotary_tables()
    queries = low(jnp.concatenate([query_raw[..., :NOPE], rotate(query_raw[..., NOPE:], cosine[:, None], sine_table[:, None])], axis=-1))
    key_latent = low_back(jnp.dot(normed, latent_down, precision=HIGHEST))
    key_low = low(rms_normed(key_latent[:, :KVR], gain_latent))
    rope_keys = low(rotate(key_latent[:, KVR:], cosine, sine_table))
    key_value = low(jnp.dot(key_low, latent_up, precision=HIGHEST)).reshape(LENGTH, H, NOPE + VD)
    block_rows = min(512, LENGTH)

    def one_block(block_number):
        query_rows = lax.dynamic_slice_in_dim(queries, block_number * block_rows, block_rows, 0)
        query_blocks = lax.dynamic_slice_in_dim(sequence_blocks, block_number * block_rows, block_rows, 0)
        return attend_rows(query_rows, key_value, rope_keys, query_blocks, sequence_blocks)
    attended = lax.map(jax.checkpoint(one_block), jnp.arange(LENGTH // block_rows, dtype=jnp.int32))
    attended = low(low_back(attended.reshape(LENGTH, H * VD)))
    branch = low_back(jnp.dot(attended, output_weight, precision=HIGHEST))
    middle = inputs + RESIDUAL_SCALE * branch
    normed_ffn = low(rms_normed(middle, gain_ffn))
    gate_pre = low_back(jnp.dot(normed_ffn, gate_weight, precision=HIGHEST))
    up_pre = low_back(jnp.dot(normed_ffn, up_weight, precision=HIGHEST))
    activated = low(jax.nn.silu(gate_pre) * up_pre)
    ffn_branch = low_back(jnp.dot(activated, down_weight, precision=HIGHEST))
    return middle + RESIDUAL_SCALE * ffn_branch

def layer_forward(inputs, weights, block_index):

    def per_sequence(loop_state, sequence_pair):
        return (loop_state, sequence_forward(sequence_pair[0], sequence_pair[1], weights))
    final_state, outputs = lax.scan(per_sequence, jnp.zeros((), jnp.float32), (inputs.reshape(SEQS, LENGTH, D), block_index))
    return outputs.reshape(TOKENS, D)

def adamw_update(master, first_moment, second_moment, gradient, learn_rate, weight_decay, is_owner):
    new_first = BETA_ONE * first_moment + (1.0 - BETA_ONE) * gradient
    new_second = BETA_TWO * second_moment + (1.0 - BETA_TWO) * gradient * gradient
    mean_hat = new_first / (1.0 - BETA_ONE ** STEP)
    square_hat = new_second / (1.0 - BETA_TWO ** STEP)
    new_master = master - learn_rate * (mean_hat / (jnp.sqrt(square_hat) + ADAM_EPS) + weight_decay * master)
    return (jnp.where(is_owner, new_master, master), jnp.where(is_owner, new_first, first_moment), jnp.where(is_owner, new_second, second_moment))

def reference(hidden, cotangent, block_index, owners, query_down, query_down_first, query_down_second, query_up, query_up_first, query_up_second, latent_down, latent_down_first, latent_down_second, latent_up, latent_up_first, latent_up_second, output_weight, output_weight_first, output_weight_second, gate_weight, gate_weight_first, gate_weight_second, up_weight, up_weight_first, up_weight_second, down_weight, down_weight_first, down_weight_second, norm_gains, norm_gains_first, norm_gains_second):
    masters = (query_down, query_up, latent_down, latent_up, output_weight, gate_weight, up_weight, down_weight, norm_gains)
    firsts = (query_down_first, query_up_first, latent_down_first, latent_up_first, output_weight_first, gate_weight_first, up_weight_first, down_weight_first, norm_gains_first)
    seconds = (query_down_second, query_up_second, latent_down_second, latent_up_second, output_weight_second, gate_weight_second, up_weight_second, down_weight_second, norm_gains_second)
    live = tuple((lax.dynamic_index_in_dim(masters[slot_number], owners[slot_number], 0, keepdims=False) for slot_number in range(9)))

    def forward(inputs, weights):
        return layer_forward(inputs, tuple((low(member) for member in weights)), block_index)
    result, pullback = jax.vjp(forward, hidden.astype(jnp.float32), live)
    input_grad, weight_grads = pullback(cotangent.astype(jnp.float32))
    learn_rates = (D ** (-0.5), QR ** (-0.5), D ** (-0.5), KVR ** (-0.5), math.sqrt(LENGTH / (0.0632 * H * VD)), D ** (-0.5), D ** (-0.5), math.sqrt(1.0 / (0.0114 * FF)), 0.6)
    decays = (WEIGHT_DECAY, WEIGHT_DECAY, WEIGHT_DECAY, WEIGHT_DECAY, WEIGHT_DECAY, WEIGHT_DECAY, WEIGHT_DECAY, WEIGHT_DECAY, 0.0)
    slot_numbers = jnp.arange(N_OWN, dtype=jnp.int32)
    updated = [result.astype(jnp.bfloat16), input_grad.astype(jnp.bfloat16)]
    for slot_number in range(9):
        gradient = weight_grads[slot_number]
        is_owner = (slot_numbers == owners[slot_number]).reshape((N_OWN,) + (1,) * gradient.ndim)
        updated.extend(adamw_update(masters[slot_number], firsts[slot_number], seconds[slot_number], gradient[None], learn_rates[slot_number], decays[slot_number], is_owner))
    return tuple(updated)
```

```python
import math

import jax
import jax.numpy as jnp
from jax import lax
from jax.experimental import pallas as pl
from jax.experimental.pallas import tpu as pltpu
from jax.sharding import PartitionSpec as P

D = 2560
H = 40
NOPE = 64
ROPE = 32
VD = 64
QR = 768
KVR = 256
FF = 6400
HEADS_STEP = 2
LANES = 128
STEP = 7


EPSILON = 1e-05
RESIDUAL_SCALE = 1.4 / math.sqrt(62.0)
BETA_ONE = 0.5
BETA_TWO = 0.55
WEIGHT_DECAY = 0.1
ADAM_EPS = 1e-08
MASKED = -1e30
SOFTMAX_SCALE = (NOPE + ROPE) ** (-0.5)


def tied(value, *earlier):
    return lax.optimization_barrier((value, *earlier))[0]


def pieces_of(rows, most):
    for parts in range(most, 1, -1):
        if rows.shape[0] % parts == 0 and (rows.shape[0] // parts) % 8 == 0:
            return [Piece(part) for part in jnp.split(rows, parts, axis=0)]
    return [Piece(rows)]


class Piece:
    def __init__(self, value):
        self.value = value
        self.leg = 0


class Line:
    def __init__(self):
        self.count, self.place = lax.axis_size("own"), lax.axis_index("own")
        self.active = []
        self.arrived = []

    def round(self, *new, after=()):
        last, half = self.count - 1, self.count // 2
        self.active.extend(new)
        values = [piece.value for piece in self.active]
        if self.arrived or after:
            values = lax.optimization_barrier((*values, *self.arrived, *after))
        self.arrived = []
        for piece, value in zip(self.active, values):
            if piece.leg < half - 1:
                hop = piece.leg
                landed = lax.ppermute(value, "own", [(hop, hop + 1), (last - hop, last - hop - 1)])
                piece.value = value + landed
            elif piece.leg == half - 1:
                landed = lax.ppermute(value, "own", [(half - 1, half), (half, half - 1)])
                piece.value = value + landed
            else:
                outer = 2 * half - 2 - piece.leg
                inner = outer + 1
                landed = lax.ppermute(
                    value, "own", [(inner, outer), (last - inner, last - outer)]
                )
                ended = (self.place == outer) | (self.place == last - outer)
                piece.value = jnp.where(ended, landed, value)
            piece.leg += 1
            self.arrived.append(landed)
        self.active = [piece for piece in self.active if piece.leg < self.count - 1]

    def then(self, value):
        return tied(value, *self.arrived)


def rows_of(pieces):
    return jnp.concatenate([piece.value for piece in pieces], axis=0)


def gather_rows(rows):
    return lax.all_gather(rows, "dp", axis=0, tiled=True)


def scatter_low(rows):
    return lax.psum_scatter(rows, "dp", scatter_dimension=0, tiled=True)


def scatter_rows(rows):
    return scatter_low(rows).astype(jnp.float32)


def rms_forward(values, norm_gain):
    inverse = lax.rsqrt(jnp.mean(values * values, axis=-1, keepdims=True) + EPSILON)
    return (values * inverse * norm_gain, inverse)


def rms_backward(values, inverse, norm_gain, grad_normed):
    normed = values * inverse
    grad_gain = jnp.sum(grad_normed * normed, axis=0)
    scaled = grad_normed * norm_gain
    grad_values = inverse * (scaled - normed * jnp.mean(scaled * normed, axis=-1, keepdims=True))
    return (grad_values, grad_gain)


def rotary_tables(positions):
    half_width = ROPE // 2
    frequency = 10000.0 ** (-jnp.arange(half_width, dtype=jnp.float32) / half_width)
    angles = positions.astype(jnp.float32)[:, None] * frequency[None, :]
    return (jnp.cos(angles), jnp.sin(angles))


def rotate(values, cosine, sine_table):
    half_width = values.shape[-1] // 2
    former = values[..., :half_width]
    latter = values[..., half_width:]
    return jnp.concatenate(
        [former * cosine - latter * sine_table, latter * cosine + former * sine_table], axis=-1
    )


def unrotate(gradient, cosine, sine_table):
    half_width = gradient.shape[-1] // 2
    former = gradient[..., :half_width]
    latter = gradient[..., half_width:]
    return jnp.concatenate(
        [former * cosine + latter * sine_table, latter * cosine - former * sine_table], axis=-1
    )


def contract_rows(first_matrix, second_matrix):
    return lax.dot_general(
        first_matrix, second_matrix, (((0,), (0,)), ((), ())), preferred_element_type=jnp.float32
    )


def times_transpose(first_matrix, second_matrix):
    return lax.dot_general(
        first_matrix, second_matrix, (((1,), (1,)), ((), ())), preferred_element_type=jnp.float32
    )


def wide_query(query):
    tokens=query.shape[1]
    zero=lambda rows: jnp.zeros((rows,tokens),query.dtype)
    return jnp.concatenate([query[:NOPE],zero(VD),query[NOPE:],zero(128-ROPE)],axis=0)

def attend_kernel(query_ref,kv_ref,rope_ref,bias_ref,out_ref,log_ref):
    rope=rope_ref[...]
    for head in range(HEADS_STEP):
        query=wide_query(query_ref[head*(NOPE+ROPE):(head+1)*(NOPE+ROPE),:])
        kv=kv_ref[:,head*(NOPE+VD):(head+1)*(NOPE+VD)]
        keys=jnp.concatenate([kv,rope],axis=1)
        scores=jnp.dot(keys,query,preferred_element_type=jnp.float32) * SOFTMAX_SCALE+bias_ref[...]
        peak=jnp.max(scores,axis=0,keepdims=True)
        exponent=jnp.exp(scores-peak)
        total=jnp.sum(exponent,axis=0,keepdims=True)
        weights=(exponent*(1.0/total)).astype(jnp.bfloat16)
        out=contract_rows(kv,weights)
        out_ref[head*VD:(head+1)*VD,:]=out[NOPE:].astype(out_ref.dtype)
        log_ref[head]=peak+jnp.log(total)

def attend(query,kv,rope,bias):
    tokens=query.shape[1]; length=kv.shape[0]
    return pl.pallas_call(
        attend_kernel,
        grid=(H//HEADS_STEP,),
        in_specs=[
            pl.BlockSpec((HEADS_STEP*(NOPE+ROPE),tokens),lambda i:(i,0)),
            pl.BlockSpec((length,HEADS_STEP*(NOPE+VD)),lambda i:(0,i)),
            pl.BlockSpec((length,128),lambda i:(0,0)),
            pl.BlockSpec((length,tokens),lambda i:(0,0)),
        ],
        out_specs=[
            pl.BlockSpec((HEADS_STEP*VD,tokens),lambda i:(i,0)),
            pl.BlockSpec((HEADS_STEP,1,tokens),lambda i:(i,0,0)),
        ],
        out_shape=[jax.ShapeDtypeStruct((H*VD,tokens),jnp.bfloat16),jax.ShapeDtypeStruct((H,1,tokens),jnp.float32)],
        compiler_params=pltpu.CompilerParams(vmem_limit_bytes=48*1024*1024),
    )(query,kv,rope,bias)

def attend_back_kernel(query_ref,kv_ref,rope_ref,bias_ref,log_ref,grad_ref,cos_ref,sin_ref,dq_ref,dkv_ref,dr_ref):
    rope=rope_ref[...]
    half=ROPE//2
    @pl.when(pl.program_id(0)==0)
    def _():
        dr_ref[...]=jnp.zeros_like(dr_ref)
    for head in range(HEADS_STEP):
        query=wide_query(query_ref[head*(NOPE+ROPE):(head+1)*(NOPE+ROPE),:])
        kv=kv_ref[:,head*(NOPE+VD):(head+1)*(NOPE+VD)]
        grad=grad_ref[head*VD:(head+1)*VD,:]
        grad=jnp.concatenate([jnp.zeros((NOPE,grad.shape[1]),grad.dtype),grad],axis=0)
        keys=jnp.concatenate([kv,rope],axis=1)
        scores=jnp.dot(keys,query,preferred_element_type=jnp.float32) * SOFTMAX_SCALE+bias_ref[...]
        weights=jnp.exp(scores-log_ref[head])
        grad_weights=jnp.dot(kv,grad,preferred_element_type=jnp.float32)
        inner=jnp.sum(weights*grad_weights,axis=0,keepdims=True)
        grad_scores=(weights*(grad_weights-inner)).astype(jnp.bfloat16)
        key_side=times_transpose(grad_scores,query) * SOFTMAX_SCALE
        dkv=key_side[:,:128]+times_transpose(weights.astype(jnp.bfloat16),grad)
        dkv_ref[:,head*(NOPE+VD):(head+1)*(NOPE+VD)]=dkv.astype(dkv_ref.dtype)
        dr_ref[...]+=key_side[:,128:]
        dq=contract_rows(keys,grad_scores) * SOFTMAX_SCALE
        former=dq[128:128+half]; latter=dq[128+half:128+ROPE]
        base=head*(NOPE+ROPE)
        dq_ref[base:base+NOPE,:]=dq[:NOPE].astype(dq_ref.dtype)
        dq_ref[base+NOPE:base+NOPE+half,:]=(former*cos_ref[...]+latter*sin_ref[...]).astype(dq_ref.dtype)
        dq_ref[base+NOPE+half:base+NOPE+ROPE,:]=(latter*cos_ref[...]-former*sin_ref[...]).astype(dq_ref.dtype)

def attend_back(query,kv,rope,bias,logs,grad,cos,sin):
    tokens=query.shape[1]; length=kv.shape[0]
    return pl.pallas_call(
        attend_back_kernel,
        grid=(H//HEADS_STEP,),
        in_specs=[
            pl.BlockSpec((HEADS_STEP*(NOPE+ROPE),tokens),lambda i:(i,0)),
            pl.BlockSpec((length,HEADS_STEP*(NOPE+VD)),lambda i:(0,i)),
            pl.BlockSpec((length,128),lambda i:(0,0)),
            pl.BlockSpec((length,tokens),lambda i:(0,0)),
            pl.BlockSpec((HEADS_STEP,1,tokens),lambda i:(i,0,0)),
            pl.BlockSpec((HEADS_STEP*VD,tokens),lambda i:(i,0)),
            pl.BlockSpec((ROPE//2,tokens),lambda i:(0,0)),
            pl.BlockSpec((ROPE//2,tokens),lambda i:(0,0)),
        ],
        out_specs=[
            pl.BlockSpec((HEADS_STEP*(NOPE+ROPE),tokens),lambda i:(i,0)),
            pl.BlockSpec((length,HEADS_STEP*(NOPE+VD)),lambda i:(0,i)),
            pl.BlockSpec((length,128),lambda i:(0,0)),
        ],
        out_shape=[jax.ShapeDtypeStruct((H*(NOPE+ROPE),tokens),jnp.bfloat16),
                   jax.ShapeDtypeStruct((length,H*(NOPE+VD)),jnp.bfloat16),
                   jax.ShapeDtypeStruct((length,128),jnp.float32)],
        compiler_params=pltpu.CompilerParams(vmem_limit_bytes=48*1024*1024),
    )(query,kv,rope,bias,logs,grad,cos,sin)


def adamw_update(master, first_moment, second_moment, gradient, learn_rate, weight_decay, is_owner):
    new_first = BETA_ONE * first_moment + (1.0 - BETA_ONE) * gradient
    new_second = BETA_TWO * second_moment + (1.0 - BETA_TWO) * gradient * gradient
    mean_hat = new_first / (1.0 - BETA_ONE**STEP)
    square_hat = new_second / (1.0 - BETA_TWO**STEP)
    new_master = master - learn_rate * (
        mean_hat / (jnp.sqrt(square_hat) + ADAM_EPS) + weight_decay * master
    )
    return (
        jnp.where(is_owner, new_master, master),
        jnp.where(is_owner, new_first, first_moment),
        jnp.where(is_owner, new_second, second_moment),
    )


def shards(
    hidden,
    cotangent,
    block_index,
    owners,
    query_down,
    query_down_first,
    query_down_second,
    query_up,
    query_up_first,
    query_up_second,
    latent_down,
    latent_down_first,
    latent_down_second,
    latent_up,
    latent_up_first,
    latent_up_second,
    output_weight,
    output_weight_first,
    output_weight_second,
    gate_weight,
    gate_weight_first,
    gate_weight_second,
    up_weight,
    up_weight_first,
    up_weight_second,
    down_weight,
    down_weight_first,
    down_weight_second,
    norm_gains,
    norm_gains_first,
    norm_gains_second,
):
    own_count = lax.axis_size("own")
    own_place = lax.axis_index("own")
    tokens_here = hidden.shape[0]
    sequence_length = tokens_here * own_count
    low = jnp.bfloat16
    inputs = hidden.astype(jnp.float32)
    is_owner = [own_place == owners[slot] for slot in range(9)]
    def owned(slot, tensor):
        return jnp.where(is_owner[slot], tensor[0], 0.0).astype(low)

    gain_count = norm_gains.shape[1]
    gain_columns = -(-gain_count // query_down.shape[1])
    gain_block = jnp.pad(
        owned(8, norm_gains), (0, gain_columns * query_down.shape[1] - gain_count)
    ).reshape(gain_columns, query_down.shape[1])
    width = QR + KVR + ROPE
    line = Line()
    down_latents = Piece(
        jnp.concatenate([owned(0, query_down), owned(2, latent_down), gain_block.T], axis=-1)
    )
    query_up_rows = Piece(owned(1, query_up))
    latent_up_rows = Piece(owned(3, latent_up))
    output_rows = Piece(owned(4, output_weight))
    gate_rows = pieces_of(owned(5, gate_weight), 2)
    up_rows = pieces_of(owned(6, up_weight), 2)
    down_rows = pieces_of(owned(7, down_weight), 2)
    grad_ffn_all = gather_rows(
        (RESIDUAL_SCALE * cotangent.astype(jnp.float32)).astype(low)
    )
    line.round(down_latents)
    line.round(query_up_rows, latent_up_rows)
    line.round()
    down_latents_all = gather_rows(down_latents.value)
    line.round(output_rows)
    query_up_all = gather_rows(query_up_rows.value)
    latent_up_all = gather_rows(latent_up_rows.value)
    down_latents_all = line.then(down_latents_all)
    line.round(gate_rows[0])
    gains_float = down_latents_all[:, width:].reshape(-1, query_down.shape[1], gain_columns)
    gains_float = gains_float.transpose(0, 2, 1).reshape(-1, gain_columns * query_down.shape[1])
    gains_float = gains_float[:, :gain_count].reshape(-1).astype(jnp.float32)
    down_latents_all = down_latents_all[:, :width]
    gain_input = gains_float[:D]
    gain_query = gains_float[D : D + QR]
    gain_latent = gains_float[D + QR : D + QR + KVR]
    gain_ffn = gains_float[D + QR + KVR :]

    grad_output = cotangent.astype(jnp.float32)

    normed, inverse_input = rms_forward(inputs, gain_input)
    normed_low = normed.astype(low)
    latents = jnp.dot(normed_low, down_latents_all, preferred_element_type=jnp.float32)
    query_latent = latents[:, :QR]
    key_latent = latents[:, QR:]
    query_normed, inverse_query = rms_forward(query_latent, gain_query)
    query_low = query_normed.astype(low)
    positions = own_place * tokens_here + jnp.arange(tokens_here, dtype=jnp.int32)
    cosine, sine_table = rotary_tables(positions)
    key_normed, inverse_key = rms_forward(key_latent[:, :KVR], gain_latent)
    key_low = key_normed.astype(low)
    rope_low = rotate(key_latent[:, KVR:], cosine, sine_table).astype(low)
    gathered_keys = lax.all_gather(
        jnp.concatenate([key_low, rope_low], axis=-1), "own", axis=0, tiled=True
    )
    line.round(*gate_rows[1:], after=[gathered_keys])
    output_all = gather_rows(output_rows.value)
    gathered_latent = gathered_keys[:, :KVR]
    rope_keys = jnp.pad(gathered_keys[:, KVR:], ((0, 0), (0, LANES - ROPE)))
    query_raw = lax.dot_general(
        query_up_all, query_low, (((0,), (1,)), ((), ())), preferred_element_type=jnp.float32
    ).reshape(H, NOPE + ROPE, tokens_here)
    cosine_rows, sine_rows = cosine.T, sine_table.T
    former, latter = jnp.split(query_raw[:, NOPE:], 2, axis=1)
    queries = jnp.concatenate(
        [
            query_raw[:, :NOPE],
            former * cosine_rows - latter * sine_rows,
            latter * cosine_rows + former * sine_rows,
        ],
        axis=1,
    )
    queries = queries.astype(low).reshape(H * (NOPE + ROPE), tokens_here)
    key_value = jnp.dot(gathered_latent, latent_up_all, preferred_element_type=jnp.float32).astype(
        low
    )
    key_value, queries = line.then(key_value), line.then(queries)
    line.round(up_rows[0], after=[key_value])
    sequence_blocks = block_index[0]
    query_blocks = lax.dynamic_slice_in_dim(
        sequence_blocks, own_place * tokens_here, tokens_here, 0
    )
    bias = jnp.where(sequence_blocks[:, None] <= query_blocks[None, :], 0.0, MASKED)
    bias = bias.astype(jnp.float32)
    attended_low, logsum = attend(queries, key_value, rope_keys, bias)
    line.round(*up_rows[1:], after=[attended_low])
    gate_columns = lax.all_to_all(rows_of(gate_rows), "dp", 1, 0, tiled=True)
    output_all = line.then(output_all)
    branch = contract_rows(attended_low, output_all)
    middle = inputs + RESIDUAL_SCALE * branch
    normed_ffn, inverse_ffn = rms_forward(middle, gain_ffn)

    normed_ffn_low = normed_ffn.astype(low)
    line.round(down_rows[0], after=[normed_ffn_low])
    normed_ffn_all = gather_rows(normed_ffn_low)
    line.round(*down_rows[1:])
    up_columns = lax.all_to_all(rows_of(up_rows), "dp", 1, 0, tiled=True)
    while line.active:
        line.round()
    down_rows = rows_of(down_rows)
    gate_pre = jnp.dot(normed_ffn_all, gate_columns, preferred_element_type=jnp.float32)
    up_pre = jnp.dot(normed_ffn_all, up_columns, preferred_element_type=jnp.float32)
    sigmoid_gate = jax.nn.sigmoid(gate_pre)
    silu_gate = gate_pre * sigmoid_gate
    activated_low = (silu_gate * up_pre).astype(low)
    down_part = contract_rows(activated_low, grad_ffn_all).astype(low)
    line = Line()
    down_sum = pieces_of(down_part, 4)
    line.round(down_sum[0])
    grad_activated = times_transpose(grad_ffn_all, down_rows)
    grad_gate_pre = (
        grad_activated * up_pre * sigmoid_gate * (1.0 + gate_pre * (1.0 - sigmoid_gate))
    ).astype(low)
    grad_up_pre = (grad_activated * silu_gate).astype(low)
    grad_normed_ffn = (
        times_transpose(grad_gate_pre, gate_columns) + times_transpose(grad_up_pre, up_columns)
    ).astype(low)
    grad_normed_ffn, grad_gate_pre, grad_up_pre = lax.optimization_barrier(
        (grad_normed_ffn, grad_gate_pre, grad_up_pre)
    )
    grad_normed_ffn = scatter_rows(grad_normed_ffn)
    line.round(*down_sum[1:2])
    gate_part = contract_rows(normed_ffn_all, grad_gate_pre).astype(low)
    gate_part, grad_up_pre = lax.optimization_barrier((gate_part, grad_up_pre))
    gate_part = lax.all_to_all(gate_part, "dp", 0, 1, tiled=True)
    line.round(*down_sum[2:3])
    grad_up_pre = line.then(grad_up_pre)
    up_part = contract_rows(normed_ffn_all, grad_up_pre).astype(low)
    line.round(*down_sum[3:4], after=[up_part])
    up_part = lax.all_to_all(tied(up_part, gate_part), "dp", 0, 1, tiled=True)
    gate_sum = pieces_of(gate_part, 2)
    line.round(gate_sum[0])
    grad_normed_ffn = line.then(grad_normed_ffn)

    grad_middle_part, grad_gain_ffn = rms_backward(middle, inverse_ffn, gain_ffn, grad_normed_ffn)
    grad_middle = grad_output + grad_middle_part
    grad_branch = (RESIDUAL_SCALE * grad_middle).astype(low)
    output_part = jnp.dot(attended_low, grad_branch, preferred_element_type=jnp.float32).astype(low)
    grad_attended = times_transpose(output_all, grad_branch).astype(low)
    grad_attended, output_part = lax.optimization_barrier((grad_attended, output_part))
    output_part = scatter_low(output_part)
    line.round(*gate_sum[1:], after=[grad_attended])
    grad_query_raw, grad_key, grad_rope = attend_back(
        queries, key_value, rope_keys, bias, logsum, grad_attended, cosine_rows, sine_rows
    )
    grad_key = line.then(grad_key)
    up_sum = pieces_of(up_part, 2)
    line.round(up_sum[0], after=[grad_query_raw])
    latent_up_part = scatter_low(contract_rows(gathered_latent, grad_key).astype(low))
    key_side = jnp.concatenate([times_transpose(grad_key, latent_up_all), grad_rope[:, :ROPE]], axis=-1)
    key_side = lax.psum_scatter(
        key_side.astype(low), "own", scatter_dimension=0, tiled=True
    ).astype(jnp.float32)
    query_up_part = scatter_low(
        lax.dot_general(
            query_low,
            grad_query_raw,
            (((0,), (1,)), ((), ())),
            preferred_element_type=jnp.float32,
        ).astype(low)
    )
    grad_query_normed = lax.dot_general(
        grad_query_raw, query_up_all, (((0,), (1,)), ((), ())), preferred_element_type=jnp.float32
    )
    grad_query_latent, grad_gain_query = rms_backward(
        query_latent, inverse_query, gain_query, grad_query_normed
    )
    grad_key_latent, grad_gain_latent = rms_backward(
        key_latent[:, :KVR], inverse_key, gain_latent, key_side[:, :KVR]
    )
    grad_latents = jnp.concatenate(
        [grad_query_latent, grad_key_latent, unrotate(key_side[:, KVR:], cosine, sine_table)],
        axis=-1,
    ).astype(low)
    grad_latents = line.then(grad_latents)
    grad_normed = times_transpose(grad_latents, down_latents_all)
    grad_inputs, grad_gain_input = rms_backward(inputs, inverse_input, gain_input, grad_normed)
    input_grad = (grad_middle + grad_inputs).astype(low)
    grad_gains = jnp.concatenate(
        [grad_gain_input, grad_gain_query, grad_gain_latent, grad_gain_ffn]
    ).reshape(-1, gain_count)
    grad_gains = jnp.pad(
        grad_gains, ((0, 0), (0, gain_columns * query_down.shape[1] - gain_count))
    ).reshape(-1, gain_columns, query_down.shape[1])
    latents_part = jnp.concatenate(
        [
            contract_rows(normed_low, grad_latents),
            grad_gains.transpose(0, 2, 1).reshape(-1, gain_columns),
        ],
        axis=-1,
    ).astype(low)
    line.round(*up_sum[1:], after=[latents_part])
    latents_part = scatter_low(latents_part)
    ffn_part = jnp.dot(activated_low, down_rows, preferred_element_type=jnp.float32).astype(low)
    ffn_branch = scatter_rows(tied(line.then(ffn_part), latents_part))
    block_output = (middle + RESIDUAL_SCALE * ffn_branch).astype(low)
    output_sum, latent_up_sum = Piece(output_part), Piece(latent_up_part)
    query_up_sum, latents_sum = Piece(query_up_part), Piece(latents_part)
    line.round(output_sum)
    line.round(latent_up_sum, query_up_sum)
    line.round(latents_sum)
    while line.active:
        line.round()
    reduced_output, reduced_latent_up = output_sum.value, latent_up_sum.value
    reduced_query_up, reduced_latents = query_up_sum.value, latents_sum.value
    reduced_down, reduced_gate, reduced_up = rows_of(down_sum), rows_of(gate_sum), rows_of(up_sum)
    reduced_latents = reduced_latents.astype(jnp.float32)
    reduced_gains = reduced_latents[:, width:].T.reshape(-1)[:gain_count]
    reduced = (
        reduced_latents[:, :QR],
        reduced_query_up.astype(jnp.float32),
        reduced_latents[:, QR:width],
        reduced_latent_up.astype(jnp.float32),
        reduced_output.astype(jnp.float32),
        reduced_gate.astype(jnp.float32),
        reduced_up.astype(jnp.float32),
        reduced_down.astype(jnp.float32),
        reduced_gains,
    )
    states = (
        (query_down, query_down_first, query_down_second),
        (query_up, query_up_first, query_up_second),
        (latent_down, latent_down_first, latent_down_second),
        (latent_up, latent_up_first, latent_up_second),
        (output_weight, output_weight_first, output_weight_second),
        (gate_weight, gate_weight_first, gate_weight_second),
        (up_weight, up_weight_first, up_weight_second),
        (down_weight, down_weight_first, down_weight_second),
        (norm_gains, norm_gains_first, norm_gains_second),
    )
    learn_rates = (
        D ** (-0.5),
        QR ** (-0.5),
        D ** (-0.5),
        KVR ** (-0.5),
        math.sqrt(sequence_length / (0.0632 * H * VD)),
        D ** (-0.5),
        D ** (-0.5),
        math.sqrt(1.0 / (0.0114 * FF)),
        0.6,
    )
    results = [block_output, input_grad]
    for slot in range(9):
        master, first_moment, second_moment = states[slot]
        updated = adamw_update(
            master[0],
            first_moment[0],
            second_moment[0],
            reduced[slot],
            learn_rates[slot],
            0.0 if slot == 8 else WEIGHT_DECAY,
            is_owner[slot],
        )
        results.extend((member[None] for member in updated))
    return tuple(results)


def solution(mesh):
    return jax.shard_map(
        shards,
        mesh=mesh,
        in_specs=(
            P(("dp", "own"), None),
            P(("dp", "own"), None),
            P("dp", None),
            P(),
            P("own", "dp", None),
            P("own", "dp", None),
            P("own", "dp", None),
            P("own", "dp", None),
            P("own", "dp", None),
            P("own", "dp", None),
            P("own", "dp", None),
            P("own", "dp", None),
            P("own", "dp", None),
            P("own", "dp", None),
            P("own", "dp", None),
            P("own", "dp", None),
            P("own", "dp", None),
            P("own", "dp", None),
            P("own", "dp", None),
            P("own", "dp", None),
            P("own", "dp", None),
            P("own", "dp", None),
            P("own", "dp", None),
            P("own", "dp", None),
            P("own", "dp", None),
            P("own", "dp", None),
            P("own", "dp", None),
            P("own", "dp", None),
            P("own", "dp"),
            P("own", "dp"),
            P("own", "dp"),
        ),
        out_specs=(
            P(("dp", "own"), None),
            P(("dp", "own"), None),
            P("own", "dp", None),
            P("own", "dp", None),
            P("own", "dp", None),
            P("own", "dp", None),
            P("own", "dp", None),
            P("own", "dp", None),
            P("own", "dp", None),
            P("own", "dp", None),
            P("own", "dp", None),
            P("own", "dp", None),
            P("own", "dp", None),
            P("own", "dp", None),
            P("own", "dp", None),
            P("own", "dp", None),
            P("own", "dp", None),
            P("own", "dp", None),
            P("own", "dp", None),
            P("own", "dp", None),
            P("own", "dp", None),
            P("own", "dp", None),
            P("own", "dp", None),
            P("own", "dp", None),
            P("own", "dp", None),
            P("own", "dp", None),
            P("own", "dp"),
            P("own", "dp"),
            P("own", "dp"),
        ),
        check_vma=False,
    )
```

```python
import math

import jax
import jax.numpy as jnp
from jax import lax
from jax.experimental import pallas as pl
from jax.experimental.pallas import tpu as pltpu
from jax.sharding import PartitionSpec as P

D = 2560
H = 40
NOPE = 64
ROPE = 32
VD = 64
QR = 768
KVR = 256
FF = 6400
GAINS = 6144
HEADS_STEP = 2
LANES = 128
STEP = 7


EPSILON = 1e-05
RESIDUAL_SCALE = 1.4 / math.sqrt(62.0)
BETA_ONE = 0.5
BETA_TWO = 0.55
WEIGHT_DECAY = 0.1
ADAM_EPS = 1e-08
MASKED = -1e30
SOFTMAX_SCALE = (NOPE + ROPE) ** (-0.5)


def tied(value, *earlier):
    return lax.optimization_barrier((value, *earlier))[0]


def pieces_of(rows, most):
    for parts in range(most, 1, -1):
        if rows.shape[0] % parts == 0 and (rows.shape[0] // parts) % 8 == 0:
            return [Piece(part) for part in jnp.split(rows, parts, axis=0)]
    return [Piece(rows)]


class Piece:
    def __init__(self, value):
        self.value = value
        self.leg = 0


class Line:
    def __init__(self):
        self.count, self.place = lax.axis_size("own"), lax.axis_index("own")
        self.active = []
        self.arrived = []

    def begin(self, *new):
        self.active.extend(new)
        values = [piece.value for piece in self.active]
        if self.arrived:
            values = lax.optimization_barrier((*values, *self.arrived))
        for piece, value in zip(self.active, values):
            piece.value = value
        self.coming = [
            lax.ppermute(piece.value, "own", self.pairs(piece.leg)) for piece in self.active
        ]

    def finish(self, *inside):
        last, half = self.count - 1, self.count // 2
        self.arrived = list(lax.optimization_barrier(tuple(self.coming)))
        for piece, arrived in zip(self.active, self.arrived):
            value = tied(piece.value, *inside) if inside else piece.value
            if piece.leg < half:
                piece.value = value + arrived
            else:
                outer = last - 1 - piece.leg
                ended = (self.place == outer) | (self.place == last - outer)
                piece.value = jnp.where(ended, arrived, value)
            piece.leg += 1
        self.active = [piece for piece in self.active if piece.leg < last]

    def round(self, *new):
        self.begin(*new)
        self.finish()

    def pairs(self, leg):
        last, half = self.count - 1, self.count // 2
        if leg == half - 1:
            return [(half - 1, half), (half, half - 1)]
        near, far = (leg, leg + 1) if leg < half else (last - leg, last - 1 - leg)
        return [(near, far), (last - near, last - far)]

    def then(self, value):
        return tied(value, *self.arrived)


def shuffled(columns):
    shares = lax.axis_size("dp")
    blocks = columns.reshape(shares, columns.shape[0] // shares, columns.shape[1])
    return lax.all_to_all(blocks, "dp", 0, 0)


def joined(blocks):
    return blocks.transpose(1, 0, 2).reshape(blocks.shape[1], -1)


def rows_of(pieces):
    return jnp.concatenate([piece.value for piece in pieces], axis=0)


def gather_rows(rows):
    return lax.all_gather(rows, "dp", axis=0, tiled=True)


def scatter_low(rows):
    return lax.psum_scatter(rows, "dp", scatter_dimension=0, tiled=True)


def scatter_rows(rows):
    return scatter_low(rows).astype(jnp.float32)


def rms_forward(values, norm_gain):
    inverse = lax.rsqrt(jnp.mean(values * values, axis=-1, keepdims=True) + EPSILON)
    return (values * inverse * norm_gain, inverse)


def rms_backward(values, inverse, norm_gain, grad_normed):
    normed = values * inverse
    grad_gain = jnp.sum(grad_normed * normed, axis=0)
    scaled = grad_normed * norm_gain
    grad_values = inverse * (scaled - normed * jnp.mean(scaled * normed, axis=-1, keepdims=True))
    return (grad_values, grad_gain)


def rotary_tables(positions):
    half_width = ROPE // 2
    frequency = 10000.0 ** (-jnp.arange(half_width, dtype=jnp.float32) / half_width)
    angles = positions.astype(jnp.float32)[:, None] * frequency[None, :]
    return (jnp.cos(angles), jnp.sin(angles))


def rotate(values, cosine, sine_table):
    half_width = values.shape[-1] // 2
    former = values[..., :half_width]
    latter = values[..., half_width:]
    return jnp.concatenate(
        [former * cosine - latter * sine_table, latter * cosine + former * sine_table], axis=-1
    )


def unrotate(gradient, cosine, sine_table):
    half_width = gradient.shape[-1] // 2
    former = gradient[..., :half_width]
    latter = gradient[..., half_width:]
    return jnp.concatenate(
        [former * cosine + latter * sine_table, latter * cosine - former * sine_table], axis=-1
    )


def contract_rows(first_matrix, second_matrix):
    return lax.dot_general(
        first_matrix, second_matrix, (((0,), (0,)), ((), ())), preferred_element_type=jnp.float32
    )


def times_transpose(first_matrix, second_matrix):
    return lax.dot_general(
        first_matrix, second_matrix, (((1,), (1,)), ((), ())), preferred_element_type=jnp.float32
    )


def wide_query(query):
    tokens=query.shape[1]
    zero=lambda rows: jnp.zeros((rows,tokens),query.dtype)
    return jnp.concatenate([query[:NOPE],zero(VD),query[NOPE:],zero(128-ROPE)],axis=0)

def attend_kernel(query_ref,kv_ref,rope_ref,bias_ref,out_ref,log_ref):
    rope=rope_ref[...]
    for head in range(HEADS_STEP):
        query=wide_query(query_ref[head*(NOPE+ROPE):(head+1)*(NOPE+ROPE),:])
        kv=kv_ref[:,head*(NOPE+VD):(head+1)*(NOPE+VD)]
        keys=jnp.concatenate([kv,rope],axis=1)
        scores=jnp.dot(keys,query,preferred_element_type=jnp.float32) * SOFTMAX_SCALE+bias_ref[...]
        peak=jnp.max(scores,axis=0,keepdims=True)
        exponent=jnp.exp(scores-peak)
        total=jnp.sum(exponent,axis=0,keepdims=True)
        weights=(exponent*(1.0/total)).astype(jnp.bfloat16)
        out=contract_rows(kv,weights)
        out_ref[head*VD:(head+1)*VD,:]=out[NOPE:].astype(out_ref.dtype)
        log_ref[head]=peak+jnp.log(total)

def attend(query,kv,rope,bias,first,heads):
    tokens=query.shape[1]; length=kv.shape[0]
    return pl.pallas_call(
        attend_kernel,
        grid=(heads//HEADS_STEP,),
        in_specs=[
            pl.BlockSpec((HEADS_STEP*(NOPE+ROPE),tokens),lambda i:(i+first//HEADS_STEP,0)),
            pl.BlockSpec((length,HEADS_STEP*(NOPE+VD)),lambda i:(0,i+first//HEADS_STEP)),
            pl.BlockSpec((length,128),lambda i:(0,0)),
            pl.BlockSpec((length,tokens),lambda i:(0,0)),
        ],
        out_specs=[
            pl.BlockSpec((HEADS_STEP*VD,tokens),lambda i:(i,0)),
            pl.BlockSpec((HEADS_STEP,1,tokens),lambda i:(i,0,0)),
        ],
        out_shape=[jax.ShapeDtypeStruct((heads*VD,tokens),jnp.bfloat16),jax.ShapeDtypeStruct((heads,1,tokens),jnp.float32)],
        compiler_params=pltpu.CompilerParams(vmem_limit_bytes=48*1024*1024),
    )(query,kv,rope,bias)

def attend_back_kernel(query_ref,kv_ref,rope_ref,bias_ref,log_ref,grad_ref,cos_ref,sin_ref,dq_ref,dkv_ref,dr_ref):
    rope=rope_ref[...]
    half=ROPE//2
    @pl.when(pl.program_id(0)==0)
    def _():
        dr_ref[...]=jnp.zeros_like(dr_ref)
    for head in range(HEADS_STEP):
        query=wide_query(query_ref[head*(NOPE+ROPE):(head+1)*(NOPE+ROPE),:])
        kv=kv_ref[:,head*(NOPE+VD):(head+1)*(NOPE+VD)]
        grad=grad_ref[head*VD:(head+1)*VD,:]
        grad=jnp.concatenate([jnp.zeros((NOPE,grad.shape[1]),grad.dtype),grad],axis=0)
        keys=jnp.concatenate([kv,rope],axis=1)
        scores=jnp.dot(keys,query,preferred_element_type=jnp.float32) * SOFTMAX_SCALE+bias_ref[...]
        weights=jnp.exp(scores-log_ref[head])
        grad_weights=jnp.dot(kv,grad,preferred_element_type=jnp.float32)
        inner=jnp.sum(weights*grad_weights,axis=0,keepdims=True)
        grad_scores=(weights*(grad_weights-inner)).astype(jnp.bfloat16)
        key_side=times_transpose(grad_scores,query) * SOFTMAX_SCALE
        dkv=key_side[:,:128]+times_transpose(weights.astype(jnp.bfloat16),grad)
        dkv_ref[:,head*(NOPE+VD):(head+1)*(NOPE+VD)]=dkv.astype(dkv_ref.dtype)
        dr_ref[...]+=key_side[:,128:]
        dq=contract_rows(keys,grad_scores) * SOFTMAX_SCALE
        former=dq[128:128+half]; latter=dq[128+half:128+ROPE]
        base=head*(NOPE+ROPE)
        dq_ref[base:base+NOPE,:]=dq[:NOPE].astype(dq_ref.dtype)
        dq_ref[base+NOPE:base+NOPE+half,:]=(former*cos_ref[...]+latter*sin_ref[...]).astype(dq_ref.dtype)
        dq_ref[base+NOPE+half:base+NOPE+ROPE,:]=(latter*cos_ref[...]-former*sin_ref[...]).astype(dq_ref.dtype)

def attend_back(query,kv,rope,bias,logs,grad,cos,sin):
    tokens=query.shape[1]; length=kv.shape[0]
    return pl.pallas_call(
        attend_back_kernel,
        grid=(H//HEADS_STEP,),
        in_specs=[
            pl.BlockSpec((HEADS_STEP*(NOPE+ROPE),tokens),lambda i:(i,0)),
            pl.BlockSpec((length,HEADS_STEP*(NOPE+VD)),lambda i:(0,i)),
            pl.BlockSpec((length,128),lambda i:(0,0)),
            pl.BlockSpec((length,tokens),lambda i:(0,0)),
            pl.BlockSpec((HEADS_STEP,1,tokens),lambda i:(i,0,0)),
            pl.BlockSpec((HEADS_STEP*VD,tokens),lambda i:(i,0)),
            pl.BlockSpec((ROPE//2,tokens),lambda i:(0,0)),
            pl.BlockSpec((ROPE//2,tokens),lambda i:(0,0)),
        ],
        out_specs=[
            pl.BlockSpec((HEADS_STEP*(NOPE+ROPE),tokens),lambda i:(i,0)),
            pl.BlockSpec((length,HEADS_STEP*(NOPE+VD)),lambda i:(0,i)),
            pl.BlockSpec((length,128),lambda i:(0,0)),
        ],
        out_shape=[jax.ShapeDtypeStruct((H*(NOPE+ROPE),tokens),jnp.bfloat16),
                   jax.ShapeDtypeStruct((length,H*(NOPE+VD)),jnp.bfloat16),
                   jax.ShapeDtypeStruct((length,128),jnp.float32)],
        compiler_params=pltpu.CompilerParams(vmem_limit_bytes=48*1024*1024),
    )(query,kv,rope,bias,logs,grad,cos,sin)


def adamw_update(master, first_moment, second_moment, gradient, learn_rate, weight_decay, is_owner):
    new_first = BETA_ONE * first_moment + (1.0 - BETA_ONE) * gradient
    new_second = BETA_TWO * second_moment + (1.0 - BETA_TWO) * gradient * gradient
    mean_hat = new_first / (1.0 - BETA_ONE**STEP)
    square_hat = new_second / (1.0 - BETA_TWO**STEP)
    new_master = master - learn_rate * (
        mean_hat / (jnp.sqrt(square_hat) + ADAM_EPS) + weight_decay * master
    )
    return (
        jnp.where(is_owner, new_master, master),
        jnp.where(is_owner, new_first, first_moment),
        jnp.where(is_owner, new_second, second_moment),
    )


def shards(
    hidden,
    cotangent,
    block_index,
    owners,
    query_down,
    query_down_first,
    query_down_second,
    query_up,
    query_up_first,
    query_up_second,
    latent_down,
    latent_down_first,
    latent_down_second,
    latent_up,
    latent_up_first,
    latent_up_second,
    output_weight,
    output_weight_first,
    output_weight_second,
    gate_weight,
    gate_weight_first,
    gate_weight_second,
    up_weight,
    up_weight_first,
    up_weight_second,
    down_weight,
    down_weight_first,
    down_weight_second,
    norm_gains,
    norm_gains_first,
    norm_gains_second,
):
    own_count = lax.axis_size("own")
    own_place = lax.axis_index("own")
    tokens_here = hidden.shape[0]
    sequence_length = tokens_here * own_count
    low = jnp.bfloat16
    inputs = hidden.astype(jnp.float32)
    is_owner = [own_place == owners[slot] for slot in range(9)]
    def owned(slot, tensor):
        return jnp.where(is_owner[slot], tensor[0], 0.0).astype(low)

    gain_count = norm_gains.shape[1]
    gain_columns = -(-gain_count // query_down.shape[1])
    gain_block = jnp.pad(
        owned(8, norm_gains), (0, gain_columns * query_down.shape[1] - gain_count)
    ).reshape(gain_columns, query_down.shape[1])
    width = QR + KVR + ROPE
    line = Line()
    down_latents = Piece(
        jnp.concatenate([owned(0, query_down), owned(2, latent_down), gain_block.T], axis=-1)
    )
    query_up_rows = Piece(owned(1, query_up))
    latent_up_rows = Piece(owned(3, latent_up))
    output_rows = Piece(owned(4, output_weight))
    gate_rows = pieces_of(owned(5, gate_weight), 2)
    up_rows = pieces_of(owned(6, up_weight), 2)
    down_rows = pieces_of(owned(7, down_weight), 2)
    grad_ffn_all = gather_rows(
        (RESIDUAL_SCALE * cotangent.astype(jnp.float32)).astype(low)
    )
    line.round(down_latents)
    line.round(query_up_rows, latent_up_rows)
    line.round(output_rows)
    down_latents_all = gather_rows(tied(down_latents.value, grad_ffn_all))
    line.round(gate_rows[0])
    query_up_all = gather_rows(query_up_rows.value)
    latent_up_all = gather_rows(latent_up_rows.value)
    down_latents_all = line.then(down_latents_all)
    gains_float = down_latents_all[:, width:].reshape(-1, query_down.shape[1], gain_columns)
    gains_float = gains_float.transpose(0, 2, 1).reshape(-1, gain_columns * query_down.shape[1])
    gains_float = gains_float[:, :gain_count].reshape(-1).astype(jnp.float32)
    down_latents_all = down_latents_all[:, :width]
    gain_input = gains_float[:D]
    gain_query = gains_float[D : D + QR]
    gain_latent = gains_float[D + QR : D + QR + KVR]
    gain_ffn = gains_float[D + QR + KVR :]

    grad_output = cotangent.astype(jnp.float32)

    normed, inverse_input = rms_forward(inputs, gain_input)
    normed_low = normed.astype(low)
    latents = jnp.dot(normed_low, down_latents_all, preferred_element_type=jnp.float32)
    query_latent = latents[:, :QR]
    key_latent = latents[:, QR:]
    query_normed, inverse_query = rms_forward(query_latent, gain_query)
    query_low = query_normed.astype(low)
    positions = own_place * tokens_here + jnp.arange(tokens_here, dtype=jnp.int32)
    cosine, sine_table = rotary_tables(positions)
    key_normed, inverse_key = rms_forward(key_latent[:, :KVR], gain_latent)
    key_low = key_normed.astype(low)
    rope_low = rotate(key_latent[:, KVR:], cosine, sine_table).astype(low)
    gathered_keys = lax.all_gather(
        jnp.concatenate([key_low, rope_low], axis=-1), "own", axis=0, tiled=True
    )
    gate_rows[-1].value = tied(gate_rows[-1].value, gathered_keys)
    line.begin(*gate_rows[1:])
    gathered_latent = gathered_keys[:, :KVR]
    rope_keys = jnp.pad(gathered_keys[:, KVR:], ((0, 0), (0, LANES - ROPE)))
    query_raw = lax.dot_general(
        query_up_all, query_low, (((0,), (1,)), ((), ())), preferred_element_type=jnp.float32
    ).reshape(H, NOPE + ROPE, tokens_here)
    cosine_rows, sine_rows = cosine.T, sine_table.T
    former, latter = jnp.split(query_raw[:, NOPE:], 2, axis=1)
    queries = jnp.concatenate(
        [
            query_raw[:, :NOPE],
            former * cosine_rows - latter * sine_rows,
            latter * cosine_rows + former * sine_rows,
        ],
        axis=1,
    )
    queries = queries.astype(low).reshape(H * (NOPE + ROPE), tokens_here)
    key_value = jnp.dot(gathered_latent, latent_up_all, preferred_element_type=jnp.float32).astype(
        low
    )
    line.finish(key_value)
    output_all = gather_rows(output_rows.value)
    sequence_blocks = block_index[0]
    query_blocks = lax.dynamic_slice_in_dim(
        sequence_blocks, own_place * tokens_here, tokens_here, 0
    )
    bias = jnp.where(sequence_blocks[:, None] <= query_blocks[None, :], 0.0, MASKED)
    bias = bias.astype(jnp.float32)
    half_heads = H // 2
    line.begin(up_rows[0])
    attended_first, logsum_first = attend(
        queries, line.then(key_value), rope_keys, bias, 0, half_heads
    )
    line.finish(attended_first)
    queries_second = line.then(queries)
    line.begin(*up_rows[1:])
    attended_second, logsum_second = attend(
        queries_second, key_value, rope_keys, bias, half_heads, H - half_heads
    )
    line.finish(attended_second)
    attended_low = line.then(jnp.concatenate([attended_first, attended_second], axis=0))
    logsum = jnp.concatenate([logsum_first, logsum_second], axis=0)
    line.begin(down_rows[0])
    branch = contract_rows(attended_low, output_all)
    middle = inputs + RESIDUAL_SCALE * branch
    normed_ffn, inverse_ffn = rms_forward(middle, gain_ffn)

    normed_ffn_low = normed_ffn.astype(low)
    line.finish(normed_ffn_low)
    normed_ffn_all = gather_rows(normed_ffn_low)
    normed_columns = lax.all_to_all(line.then(normed_low), "dp", 1, 0, tiled=True)
    gate_rows = line.then(rows_of(gate_rows))
    line.begin(*down_rows[1:])
    gate_columns = lax.all_to_all(gate_rows, "dp", 1, 0, tiled=True)
    line.finish()
    line.begin()
    up_columns = lax.all_to_all(line.then(rows_of(up_rows)), "dp", 1, 0, tiled=True)
    line.finish(normed_ffn_all, gate_columns)
    line.begin()
    gate_pre = jnp.dot(
        line.then(normed_ffn_all), gate_columns, preferred_element_type=jnp.float32
    )
    line.finish(gate_pre, up_columns)
    down_rows = rows_of(down_rows)
    up_pre = jnp.dot(normed_ffn_all, up_columns, preferred_element_type=jnp.float32)
    sigmoid_gate = jax.nn.sigmoid(gate_pre)
    silu_gate = gate_pre * sigmoid_gate
    activated_low = (silu_gate * up_pre).astype(low)
    down_part = contract_rows(activated_low, grad_ffn_all).astype(low)
    line = Line()
    down_sum = pieces_of(down_part, 2)
    line.begin(down_sum[0])
    grad_activated = times_transpose(tied(grad_ffn_all, down_part), down_rows)
    grad_gate_pre = (
        grad_activated * up_pre * sigmoid_gate * (1.0 + gate_pre * (1.0 - sigmoid_gate))
    ).astype(low)
    grad_up_pre = (grad_activated * silu_gate).astype(low)
    line.finish(grad_gate_pre, grad_up_pre)
    grad_gate_pre = line.then(grad_gate_pre)
    line.begin(*down_sum[1:2])
    grad_normed_ffn = (
        times_transpose(grad_gate_pre, gate_columns) + times_transpose(grad_up_pre, up_columns)
    ).astype(low)
    gate_part = contract_rows(normed_ffn_all, tied(grad_gate_pre, grad_normed_ffn)).astype(low)
    line.finish(grad_normed_ffn, gate_part)
    grad_normed_ffn = scatter_rows(grad_normed_ffn)
    gate_sum = pieces_of(gate_part, 2)
    grad_up_pre = line.then(grad_up_pre)
    line.begin(gate_sum[0])
    up_part = contract_rows(normed_ffn_all, grad_up_pre).astype(low)
    line.finish(up_part)
    up_sum = pieces_of(up_part, 2)
    grad_normed_ffn = line.then(grad_normed_ffn)
    line.begin(*gate_sum[1:])

    grad_middle_part, grad_gain_ffn = rms_backward(middle, inverse_ffn, gain_ffn, grad_normed_ffn)
    grad_middle = grad_output + grad_middle_part
    grad_branch = (RESIDUAL_SCALE * grad_middle).astype(low)
    output_part = jnp.dot(attended_low, grad_branch, preferred_element_type=jnp.float32).astype(low)
    grad_attended = times_transpose(output_all, grad_branch).astype(low)
    grad_attended, output_part = lax.optimization_barrier((grad_attended, output_part))
    output_part = scatter_low(output_part)
    line.finish(grad_attended)
    queries_again = line.then(queries)
    line.begin(up_sum[0])
    grad_query_raw, grad_key, grad_rope = attend_back(
        queries_again, key_value, rope_keys, bias, logsum, grad_attended, cosine_rows, sine_rows
    )
    line.finish(grad_query_raw)
    grad_key, grad_query_raw = line.then(grad_key), line.then(grad_query_raw)
    line.begin(*up_sum[1:])
    states = (
        (query_down, query_down_first, query_down_second),
        (query_up, query_up_first, query_up_second),
        (latent_down, latent_down_first, latent_down_second),
        (latent_up, latent_up_first, latent_up_second),
        (output_weight, output_weight_first, output_weight_second),
        (gate_weight, gate_weight_first, gate_weight_second),
        (up_weight, up_weight_first, up_weight_second),
        (down_weight, down_weight_first, down_weight_second),
        (norm_gains, norm_gains_first, norm_gains_second),
    )
    learn_rates = (
        D ** (-0.5),
        QR ** (-0.5),
        D ** (-0.5),
        KVR ** (-0.5),
        math.sqrt(sequence_length / (0.0632 * H * VD)),
        D ** (-0.5),
        D ** (-0.5),
        math.sqrt(1.0 / (0.0114 * FF)),
        0.6,
    )

    def update(slot, gradient):
        master, first_moment, second_moment = states[slot]
        return adamw_update(
            master[0],
            first_moment[0],
            second_moment[0],
            gradient.astype(jnp.float32),
            learn_rates[slot],
            0.0 if slot == 8 else WEIGHT_DECAY,
            is_owner[slot],
        )

    new_down = update(7, line.then(rows_of(down_sum)))
    key_side = jnp.concatenate([times_transpose(grad_key, latent_up_all), grad_rope[:, :ROPE]], axis=-1)
    key_side = lax.psum_scatter(
        tied(key_side.astype(low), output_part), "own", scatter_dimension=0, tiled=True
    ).astype(jnp.float32)
    latent_up_part = contract_rows(gathered_latent, grad_key).astype(low)
    query_up_part = lax.dot_general(
        query_low, grad_query_raw, (((0,), (1,)), ((), ())), preferred_element_type=jnp.float32
    ).astype(low)
    latent_up_part, query_up_part = scatter_low(latent_up_part), scatter_low(query_up_part)
    grad_query_normed = lax.dot_general(
        grad_query_raw, query_up_all, (((0,), (1,)), ((), ())), preferred_element_type=jnp.float32
    )
    grad_query_latent, grad_gain_query = rms_backward(
        query_latent, inverse_query, gain_query, grad_query_normed
    )
    line.finish(grad_query_latent, *new_down)
    output_sum = Piece(output_part)
    line.begin(output_sum)
    gate_blocks = shuffled(rows_of(gate_sum))
    line.finish()
    key_side = line.then(key_side)
    grad_key_latent, grad_gain_latent = rms_backward(
        key_latent[:, :KVR], inverse_key, gain_latent, key_side[:, :KVR]
    )
    grad_latents = jnp.concatenate(
        [grad_query_latent, grad_key_latent, unrotate(key_side[:, KVR:], cosine, sine_table)],
        axis=-1,
    ).astype(low)
    grad_normed = times_transpose(grad_latents, down_latents_all)
    grad_inputs, grad_gain_input = rms_backward(inputs, inverse_input, gain_input, grad_normed)
    input_grad = (grad_middle + grad_inputs).astype(low)
    gain_width = -(-GAINS // tokens_here)
    grad_gains = jnp.concatenate(
        [grad_gain_input, grad_gain_query, grad_gain_latent, grad_gain_ffn]
    )
    grad_gains = jnp.pad(grad_gains, (0, gain_width * tokens_here - GAINS))
    grad_latents_all = gather_rows(
        jnp.concatenate(
            [grad_latents, grad_gains.reshape(tokens_here, gain_width).astype(low)], axis=-1
        )
    )
    activated_late = line.then(activated_low)
    latent_up_sum, query_up_sum = Piece(latent_up_part), Piece(query_up_part)
    line.begin(latent_up_sum, query_up_sum)
    ffn_part = jnp.dot(activated_late, down_rows, preferred_element_type=jnp.float32).astype(low)
    line.finish(ffn_part, gate_blocks)
    up_blocks = shuffled(rows_of(up_sum))
    gate_gradient = joined(line.then(gate_blocks))
    ffn_branch = scatter_rows(tied(line.then(ffn_part), grad_latents_all))
    block_output = (middle + RESIDUAL_SCALE * ffn_branch).astype(low)
    latents_part = contract_rows(normed_columns, grad_latents_all[:, :width])
    grad_gains = grad_latents_all[:, width:].astype(jnp.float32)
    grad_gains = jnp.sum(grad_gains.reshape(-1, tokens_here * gain_width), axis=0)
    grad_gains = lax.dynamic_slice_in_dim(
        grad_gains, lax.axis_index("dp") * gain_count, gain_count, 0
    )
    grad_gains = jnp.pad(
        grad_gains, (0, gain_columns * query_down.shape[1] - gain_count)
    ).reshape(gain_columns, query_down.shape[1])
    latents_sum = Piece(jnp.concatenate([latents_part, grad_gains.T], axis=-1).astype(low))
    line.begin(latents_sum)
    line.finish(input_grad)
    line.begin()
    line.finish(up_blocks)
    up_gradient = joined(line.then(up_blocks))
    while line.active:
        line.round()
    reduced_output, reduced_latents = output_sum.value, latents_sum.value

    reduced_latent_up, reduced_query_up = latent_up_sum.value, query_up_sum.value
    reduced_gate, reduced_up = gate_gradient, up_gradient
    reduced_latents = reduced_latents.astype(jnp.float32)
    reduced_gains = reduced_latents[:, width:].T.reshape(-1)[:gain_count]
    reduced = (
        reduced_latents[:, :QR],
        reduced_query_up.astype(jnp.float32),
        reduced_latents[:, QR:width],
        reduced_latent_up.astype(jnp.float32),
        reduced_output.astype(jnp.float32),
        reduced_gate.astype(jnp.float32),
        reduced_up.astype(jnp.float32),
        None,
        reduced_gains,
    )
    results = [block_output, input_grad]
    for slot in range(9):
        updated = new_down if slot == 7 else update(slot, reduced[slot])
        results.extend((member[None] for member in updated))
    return tuple(results)


def solution(mesh):
    return jax.shard_map(
        shards,
        mesh=mesh,
        in_specs=(
            P(("dp", "own"), None),
            P(("dp", "own"), None),
            P("dp", None),
            P(),
            P("own", "dp", None),
            P("own", "dp", None),
            P("own", "dp", None),
            P("own", "dp", None),
            P("own", "dp", None),
            P("own", "dp", None),
            P("own", "dp", None),
            P("own", "dp", None),
            P("own", "dp", None),
            P("own", "dp", None),
            P("own", "dp", None),
            P("own", "dp", None),
            P("own", "dp", None),
            P("own", "dp", None),
            P("own", "dp", None),
            P("own", "dp", None),
            P("own", "dp", None),
            P("own", "dp", None),
            P("own", "dp", None),
            P("own", "dp", None),
            P("own", "dp", None),
            P("own", "dp", None),
            P("own", "dp", None),
            P("own", "dp", None),
            P("own", "dp"),
            P("own", "dp"),
            P("own", "dp"),
        ),
        out_specs=(
            P(("dp", "own"), None),
            P(("dp", "own"), None),
            P("own", "dp", None),
            P("own", "dp", None),
            P("own", "dp", None),
            P("own", "dp", None),
            P("own", "dp", None),
            P("own", "dp", None),
            P("own", "dp", None),
            P("own", "dp", None),
            P("own", "dp", None),
            P("own", "dp", None),
            P("own", "dp", None),
            P("own", "dp", None),
            P("own", "dp", None),
            P("own", "dp", None),
            P("own", "dp", None),
            P("own", "dp", None),
            P("own", "dp", None),
            P("own", "dp", None),
            P("own", "dp", None),
            P("own", "dp", None),
            P("own", "dp", None),
            P("own", "dp", None),
            P("own", "dp", None),
            P("own", "dp", None),
            P("own", "dp"),
            P("own", "dp"),
            P("own", "dp"),
        ),
        check_vma=False,
    )
```

```python
import functools
import math

import jax
import jax.numpy as jnp
from jax import lax
from jax.experimental import pallas as pl
from jax.experimental.pallas import tpu as pltpu
from jax.sharding import PartitionSpec as P

D = 2560
H = 40
NOPE = 64
ROPE = 32
VD = 64
QR = 768
KVR = 256
FF = 6400
GAINS = 6144
HEADS_STEP = 2
LANES = 128
STEP = 7


EPSILON = 1e-05
RESIDUAL_SCALE = 1.4 / math.sqrt(62.0)
BETA_ONE = 0.5
BETA_TWO = 0.55
WEIGHT_DECAY = 0.1
ADAM_EPS = 1e-08
MASKED = -1e30
SOFTMAX_SCALE = (NOPE + ROPE) ** (-0.5)


def tied(value, *earlier):
    return lax.optimization_barrier((value, *earlier))[0]


def pieces_of(rows, most):
    for parts in range(most, 1, -1):
        if rows.shape[0] % parts == 0 and (rows.shape[0] // parts) % 8 == 0:
            return [Piece(part) for part in jnp.split(rows, parts, axis=0)]
    return [Piece(rows)]


class Piece:
    def __init__(self, value):
        self.value = value
        self.leg = 0


class Line:
    def __init__(self):
        self.count, self.place = lax.axis_size("own"), lax.axis_index("own")
        self.active = []
        self.arrived = []

    def begin(self, *new):
        self.active.extend(new)
        values = [piece.value for piece in self.active]
        if self.arrived:
            values = lax.optimization_barrier((*values, *self.arrived))
        for piece, value in zip(self.active, values):
            piece.value = value
        self.coming = [
            lax.ppermute(piece.value, "own", self.pairs(piece.leg)) for piece in self.active
        ]

    def finish(self, *inside):
        last, half = self.count - 1, self.count // 2
        self.arrived = list(lax.optimization_barrier(tuple(self.coming)))
        for piece, arrived in zip(self.active, self.arrived):
            value = tied(piece.value, *inside) if inside else piece.value
            if piece.leg < half:
                piece.value = value + arrived
            else:
                outer = last - 1 - piece.leg
                ended = (self.place == outer) | (self.place == last - outer)
                piece.value = jnp.where(ended, arrived, value)
            piece.leg += 1
        self.active = [piece for piece in self.active if piece.leg < last]

    def round(self, *new):
        self.begin(*new)
        self.finish()

    def pairs(self, leg):
        last, half = self.count - 1, self.count // 2
        if leg == half - 1:
            return [(half - 1, half), (half, half - 1)]
        near, far = (leg, leg + 1) if leg < half else (last - leg, last - 1 - leg)
        return [(near, far), (last - near, last - far)]

    def then(self, value):
        return tied(value, *self.arrived)


def shuffled(columns):
    shares = lax.axis_size("dp")
    blocks = columns.reshape(shares, columns.shape[0] // shares, columns.shape[1])
    return lax.all_to_all(blocks, "dp", 0, 0)


def update_kernel(
    learn_rate,
    weight_decay,
    owner_ref,
    blocks_ref,
    master_ref,
    first_ref,
    second_ref,
    new_master_ref,
    new_first_ref,
    new_second_ref,
    gradient_ref,
):
    @pl.when(owner_ref[0] == 1)
    def _():
        width = blocks_ref.shape[2]
        for number in range(blocks_ref.shape[0]):
            gradient_ref[:, number * width : (number + 1) * width] = blocks_ref[number].astype(
                jnp.float32
            )
        gradient, master = gradient_ref[...], master_ref[...]
        new_first = BETA_ONE * first_ref[...] + (1.0 - BETA_ONE) * gradient
        new_second = BETA_TWO * second_ref[...] + (1.0 - BETA_TWO) * gradient * gradient
        mean_hat = new_first / (1.0 - BETA_ONE**STEP)
        square_hat = new_second / (1.0 - BETA_TWO**STEP)
        new_master_ref[...] = master - learn_rate * (
            mean_hat / (jnp.sqrt(square_hat) + ADAM_EPS) + weight_decay * master
        )
        new_first_ref[...] = new_first
        new_second_ref[...] = new_second

    @pl.when(owner_ref[0] != 1)
    def _():
        new_master_ref[...] = master_ref[...]
        new_first_ref[...] = first_ref[...]
        new_second_ref[...] = second_ref[...]


def update_joined(is_owner, blocks, master, first_moment, second_moment, learn_rate):
    rows, columns = master.shape
    step_rows = next(size for size in (64, 32, 16, rows) if rows % size == 0)
    state = pl.BlockSpec((step_rows, columns), lambda i, _: (i, 0))
    return pl.pallas_call(
        functools.partial(update_kernel, learn_rate, WEIGHT_DECAY),
        grid_spec=pltpu.PrefetchScalarGridSpec(
            num_scalar_prefetch=1,
            grid=(rows // step_rows,),
            in_specs=[
                pl.BlockSpec((blocks.shape[0], step_rows, blocks.shape[2]), lambda i, _: (0, i, 0)),
                state,
                state,
                state,
            ],
            out_specs=[state, state, state],
            scratch_shapes=[pltpu.VMEM((step_rows, columns), jnp.float32)],
        ),
        out_shape=[jax.ShapeDtypeStruct(master.shape, jnp.float32)] * 3,
        cost_estimate=pl.CostEstimate(
            flops=20 * rows * columns, bytes_accessed=26 * rows * columns, transcendentals=0
        ),
        compiler_params=pltpu.CompilerParams(vmem_limit_bytes=48 * 1024 * 1024),
    )(is_owner.astype(jnp.int32).reshape(1), blocks, master, first_moment, second_moment)


def rows_of(pieces):
    return jnp.concatenate([piece.value for piece in pieces], axis=0)


def gather_rows(rows):
    return lax.all_gather(rows, "dp", axis=0, tiled=True)


def scatter_low(rows):
    return lax.psum_scatter(rows, "dp", scatter_dimension=0, tiled=True)


def scatter_rows(rows):
    return scatter_low(rows).astype(jnp.float32)


def rms_forward(values, norm_gain):
    inverse = lax.rsqrt(jnp.mean(values * values, axis=-1, keepdims=True) + EPSILON)
    return (values * inverse * norm_gain, inverse)


def rms_backward(values, inverse, norm_gain, grad_normed):
    normed = values * inverse
    grad_gain = jnp.sum(grad_normed * normed, axis=0)
    scaled = grad_normed * norm_gain
    grad_values = inverse * (scaled - normed * jnp.mean(scaled * normed, axis=-1, keepdims=True))
    return (grad_values, grad_gain)


def rotary_tables(positions):
    half_width = ROPE // 2
    frequency = 10000.0 ** (-jnp.arange(half_width, dtype=jnp.float32) / half_width)
    angles = positions.astype(jnp.float32)[:, None] * frequency[None, :]
    return (jnp.cos(angles), jnp.sin(angles))


def rotate(values, cosine, sine_table):
    half_width = values.shape[-1] // 2
    former = values[..., :half_width]
    latter = values[..., half_width:]
    return jnp.concatenate(
        [former * cosine - latter * sine_table, latter * cosine + former * sine_table], axis=-1
    )


def unrotate(gradient, cosine, sine_table):
    half_width = gradient.shape[-1] // 2
    former = gradient[..., :half_width]
    latter = gradient[..., half_width:]
    return jnp.concatenate(
        [former * cosine + latter * sine_table, latter * cosine - former * sine_table], axis=-1
    )


def contract_rows(first_matrix, second_matrix):
    return lax.dot_general(
        first_matrix, second_matrix, (((0,), (0,)), ((), ())), preferred_element_type=jnp.float32
    )


def times_transpose(first_matrix, second_matrix):
    return lax.dot_general(
        first_matrix, second_matrix, (((1,), (1,)), ((), ())), preferred_element_type=jnp.float32
    )


def wide_query(query):
    tokens=query.shape[1]
    zero=lambda rows: jnp.zeros((rows,tokens),query.dtype)
    return jnp.concatenate([query[:NOPE],zero(VD),query[NOPE:],zero(128-ROPE)],axis=0)

def attend_kernel(query_ref,kv_ref,rope_ref,bias_ref,out_ref,log_ref):
    rope=rope_ref[...]
    for head in range(HEADS_STEP):
        query=wide_query(query_ref[head*(NOPE+ROPE):(head+1)*(NOPE+ROPE),:])
        kv=kv_ref[:,head*(NOPE+VD):(head+1)*(NOPE+VD)]
        keys=jnp.concatenate([kv,rope],axis=1)
        scores=jnp.dot(keys,query,preferred_element_type=jnp.float32) * SOFTMAX_SCALE+bias_ref[...]
        peak=jnp.max(scores,axis=0,keepdims=True)
        exponent=jnp.exp(scores-peak)
        total=jnp.sum(exponent,axis=0,keepdims=True)
        weights=(exponent*(1.0/total)).astype(jnp.bfloat16)
        out=contract_rows(kv,weights)
        out_ref[head*VD:(head+1)*VD,:]=out[NOPE:].astype(out_ref.dtype)
        log_ref[head]=peak+jnp.log(total)

def attend(query,kv,rope,bias,first,heads):
    tokens=query.shape[1]; length=kv.shape[0]
    return pl.pallas_call(
        attend_kernel,
        grid=(heads//HEADS_STEP,),
        in_specs=[
            pl.BlockSpec((HEADS_STEP*(NOPE+ROPE),tokens),lambda i:(i+first//HEADS_STEP,0)),
            pl.BlockSpec((length,HEADS_STEP*(NOPE+VD)),lambda i:(0,i+first//HEADS_STEP)),
            pl.BlockSpec((length,128),lambda i:(0,0)),
            pl.BlockSpec((length,tokens),lambda i:(0,0)),
        ],
        out_specs=[
            pl.BlockSpec((HEADS_STEP*VD,tokens),lambda i:(i,0)),
            pl.BlockSpec((HEADS_STEP,1,tokens),lambda i:(i,0,0)),
        ],
        out_shape=[jax.ShapeDtypeStruct((heads*VD,tokens),jnp.bfloat16),jax.ShapeDtypeStruct((heads,1,tokens),jnp.float32)],
        compiler_params=pltpu.CompilerParams(vmem_limit_bytes=48*1024*1024),
    )(query,kv,rope,bias)

def attend_back_kernel(query_ref,kv_ref,rope_ref,bias_ref,log_ref,grad_ref,cos_ref,sin_ref,dq_ref,dkv_ref,dr_ref):
    rope=rope_ref[...]
    half=ROPE//2
    @pl.when(pl.program_id(0)==0)
    def _():
        dr_ref[...]=jnp.zeros_like(dr_ref)
    for head in range(HEADS_STEP):
        query=wide_query(query_ref[head*(NOPE+ROPE):(head+1)*(NOPE+ROPE),:])
        kv=kv_ref[:,head*(NOPE+VD):(head+1)*(NOPE+VD)]
        grad=grad_ref[head*VD:(head+1)*VD,:]
        grad=jnp.concatenate([jnp.zeros((NOPE,grad.shape[1]),grad.dtype),grad],axis=0)
        keys=jnp.concatenate([kv,rope],axis=1)
        scores=jnp.dot(keys,query,preferred_element_type=jnp.float32) * SOFTMAX_SCALE+bias_ref[...]
        weights=jnp.exp(scores-log_ref[head])
        grad_weights=jnp.dot(kv,grad,preferred_element_type=jnp.float32)
        inner=jnp.sum(weights*grad_weights,axis=0,keepdims=True)
        grad_scores=(weights*(grad_weights-inner)).astype(jnp.bfloat16)
        key_side=times_transpose(grad_scores,query) * SOFTMAX_SCALE
        dkv=key_side[:,:128]+times_transpose(weights.astype(jnp.bfloat16),grad)
        dkv_ref[:,head*(NOPE+VD):(head+1)*(NOPE+VD)]=dkv.astype(dkv_ref.dtype)
        dr_ref[...]+=key_side[:,128:]
        dq=contract_rows(keys,grad_scores) * SOFTMAX_SCALE
        former=dq[128:128+half]; latter=dq[128+half:128+ROPE]
        base=head*(NOPE+ROPE)
        dq_ref[base:base+NOPE,:]=dq[:NOPE].astype(dq_ref.dtype)
        dq_ref[base+NOPE:base+NOPE+half,:]=(former*cos_ref[...]+latter*sin_ref[...]).astype(dq_ref.dtype)
        dq_ref[base+NOPE+half:base+NOPE+ROPE,:]=(latter*cos_ref[...]-former*sin_ref[...]).astype(dq_ref.dtype)

def attend_back(query,kv,rope,bias,logs,grad,cos,sin):
    tokens=query.shape[1]; length=kv.shape[0]
    return pl.pallas_call(
        attend_back_kernel,
        grid=(H//HEADS_STEP,),
        in_specs=[
            pl.BlockSpec((HEADS_STEP*(NOPE+ROPE),tokens),lambda i:(i,0)),
            pl.BlockSpec((length,HEADS_STEP*(NOPE+VD)),lambda i:(0,i)),
            pl.BlockSpec((length,128),lambda i:(0,0)),
            pl.BlockSpec((length,tokens),lambda i:(0,0)),
            pl.BlockSpec((HEADS_STEP,1,tokens),lambda i:(i,0,0)),
            pl.BlockSpec((HEADS_STEP*VD,tokens),lambda i:(i,0)),
            pl.BlockSpec((ROPE//2,tokens),lambda i:(0,0)),
            pl.BlockSpec((ROPE//2,tokens),lambda i:(0,0)),
        ],
        out_specs=[
            pl.BlockSpec((HEADS_STEP*(NOPE+ROPE),tokens),lambda i:(i,0)),
            pl.BlockSpec((length,HEADS_STEP*(NOPE+VD)),lambda i:(0,i)),
            pl.BlockSpec((length,128),lambda i:(0,0)),
        ],
        out_shape=[jax.ShapeDtypeStruct((H*(NOPE+ROPE),tokens),jnp.bfloat16),
                   jax.ShapeDtypeStruct((length,H*(NOPE+VD)),jnp.bfloat16),
                   jax.ShapeDtypeStruct((length,128),jnp.float32)],
        compiler_params=pltpu.CompilerParams(vmem_limit_bytes=48*1024*1024),
    )(query,kv,rope,bias,logs,grad,cos,sin)


def adamw_update(master, first_moment, second_moment, gradient, learn_rate, weight_decay, is_owner):
    new_first = BETA_ONE * first_moment + (1.0 - BETA_ONE) * gradient
    new_second = BETA_TWO * second_moment + (1.0 - BETA_TWO) * gradient * gradient
    mean_hat = new_first / (1.0 - BETA_ONE**STEP)
    square_hat = new_second / (1.0 - BETA_TWO**STEP)
    new_master = master - learn_rate * (
        mean_hat / (jnp.sqrt(square_hat) + ADAM_EPS) + weight_decay * master
    )
    return (
        jnp.where(is_owner, new_master, master),
        jnp.where(is_owner, new_first, first_moment),
        jnp.where(is_owner, new_second, second_moment),
    )


def shards(
    hidden,
    cotangent,
    block_index,
    owners,
    query_down,
    query_down_first,
    query_down_second,
    query_up,
    query_up_first,
    query_up_second,
    latent_down,
    latent_down_first,
    latent_down_second,
    latent_up,
    latent_up_first,
    latent_up_second,
    output_weight,
    output_weight_first,
    output_weight_second,
    gate_weight,
    gate_weight_first,
    gate_weight_second,
    up_weight,
    up_weight_first,
    up_weight_second,
    down_weight,
    down_weight_first,
    down_weight_second,
    norm_gains,
    norm_gains_first,
    norm_gains_second,
):
    own_count = lax.axis_size("own")
    own_place = lax.axis_index("own")
    tokens_here = hidden.shape[0]
    sequence_length = tokens_here * own_count
    low = jnp.bfloat16
    inputs = hidden.astype(jnp.float32)
    is_owner = [own_place == owners[slot] for slot in range(9)]
    def owned(slot, tensor):
        return jnp.where(is_owner[slot], tensor[0], 0.0).astype(low)

    gain_count = norm_gains.shape[1]
    gain_columns = -(-gain_count // query_down.shape[1])
    gain_block = jnp.pad(
        owned(8, norm_gains), (0, gain_columns * query_down.shape[1] - gain_count)
    ).reshape(gain_columns, query_down.shape[1])
    width = QR + KVR + ROPE
    line = Line()
    down_latents = Piece(
        jnp.concatenate([owned(0, query_down), owned(2, latent_down), gain_block.T], axis=-1)
    )
    query_up_rows = Piece(owned(1, query_up))
    latent_up_rows = Piece(owned(3, latent_up))
    output_rows = Piece(owned(4, output_weight))
    gate_rows = pieces_of(owned(5, gate_weight), 2)
    up_rows = pieces_of(owned(6, up_weight), 2)
    down_rows = pieces_of(owned(7, down_weight), 2)
    grad_ffn_all = gather_rows(
        (RESIDUAL_SCALE * cotangent.astype(jnp.float32)).astype(low)
    )
    line.round(down_latents)
    line.begin(query_up_rows, latent_up_rows)
    line.finish(output_rows.value, *[piece.value for piece in gate_rows])
    line.begin(output_rows)
    line.finish(*[piece.value for piece in up_rows + down_rows])
    down_latents_all = gather_rows(tied(down_latents.value, grad_ffn_all))
    line.round(gate_rows[0])
    query_up_all = gather_rows(query_up_rows.value)
    latent_up_all = gather_rows(latent_up_rows.value)
    down_latents_all = line.then(down_latents_all)
    gains_float = down_latents_all[:, width:].reshape(-1, query_down.shape[1], gain_columns)
    gains_float = gains_float.transpose(0, 2, 1).reshape(-1, gain_columns * query_down.shape[1])
    gains_float = gains_float[:, :gain_count].reshape(-1).astype(jnp.float32)
    down_latents_all = down_latents_all[:, :width]
    gain_input = gains_float[:D]
    gain_query = gains_float[D : D + QR]
    gain_latent = gains_float[D + QR : D + QR + KVR]
    gain_ffn = gains_float[D + QR + KVR :]

    grad_output = cotangent.astype(jnp.float32)

    normed, inverse_input = rms_forward(inputs, gain_input)
    normed_low = normed.astype(low)
    latents = jnp.dot(normed_low, down_latents_all, preferred_element_type=jnp.float32)
    query_latent = latents[:, :QR]
    key_latent = latents[:, QR:]
    query_normed, inverse_query = rms_forward(query_latent, gain_query)
    query_low = query_normed.astype(low)
    positions = own_place * tokens_here + jnp.arange(tokens_here, dtype=jnp.int32)
    cosine, sine_table = rotary_tables(positions)
    key_normed, inverse_key = rms_forward(key_latent[:, :KVR], gain_latent)
    key_low = key_normed.astype(low)
    rope_low = rotate(key_latent[:, KVR:], cosine, sine_table).astype(low)
    gathered_keys = lax.all_gather(
        jnp.concatenate([key_low, rope_low], axis=-1), "own", axis=0, tiled=True
    )
    gate_rows[-1].value = tied(gate_rows[-1].value, gathered_keys)
    line.begin(*gate_rows[1:])
    gathered_latent = gathered_keys[:, :KVR]
    rope_keys = jnp.pad(gathered_keys[:, KVR:], ((0, 0), (0, LANES - ROPE)))
    query_raw = lax.dot_general(
        query_up_all, query_low, (((0,), (1,)), ((), ())), preferred_element_type=jnp.float32
    ).reshape(H, NOPE + ROPE, tokens_here)
    cosine_rows, sine_rows = cosine.T, sine_table.T
    former, latter = jnp.split(query_raw[:, NOPE:], 2, axis=1)
    queries = jnp.concatenate(
        [
            query_raw[:, :NOPE],
            former * cosine_rows - latter * sine_rows,
            latter * cosine_rows + former * sine_rows,
        ],
        axis=1,
    )
    queries = queries.astype(low).reshape(H * (NOPE + ROPE), tokens_here)
    key_value = jnp.dot(gathered_latent, latent_up_all, preferred_element_type=jnp.float32).astype(
        low
    )
    line.finish(key_value)
    output_all = gather_rows(output_rows.value)
    sequence_blocks = block_index[0]
    query_blocks = lax.dynamic_slice_in_dim(
        sequence_blocks, own_place * tokens_here, tokens_here, 0
    )
    bias = jnp.where(sequence_blocks[:, None] <= query_blocks[None, :], 0.0, MASKED)
    bias = bias.astype(jnp.float32)
    half_heads = H // 2
    line.begin(up_rows[0])
    attended_first, logsum_first = attend(
        queries, line.then(key_value), rope_keys, bias, 0, half_heads
    )
    line.finish(attended_first)
    queries_second = line.then(queries)
    line.begin(*up_rows[1:])
    attended_second, logsum_second = attend(
        queries_second, key_value, rope_keys, bias, half_heads, H - half_heads
    )
    line.finish(attended_second)
    attended_low = line.then(jnp.concatenate([attended_first, attended_second], axis=0))
    logsum = jnp.concatenate([logsum_first, logsum_second], axis=0)
    line.begin(down_rows[0])
    branch = contract_rows(attended_low, output_all)
    middle = inputs + RESIDUAL_SCALE * branch
    normed_ffn, inverse_ffn = rms_forward(middle, gain_ffn)

    normed_ffn_low = normed_ffn.astype(low)
    line.finish(normed_ffn_low)
    normed_ffn_all = gather_rows(normed_ffn_low)
    normed_columns = lax.all_to_all(line.then(normed_low), "dp", 1, 0, tiled=True)
    gate_rows = line.then(rows_of(gate_rows))
    line.begin(*down_rows[1:])
    gate_columns = lax.all_to_all(gate_rows, "dp", 1, 0, tiled=True)
    line.finish()
    line.begin()
    up_columns = lax.all_to_all(line.then(rows_of(up_rows)), "dp", 1, 0, tiled=True)
    line.finish(normed_ffn_all, gate_columns, normed_columns)
    line.begin()
    gate_pre = jnp.dot(
        line.then(normed_ffn_all), gate_columns, preferred_element_type=jnp.float32
    )
    line.finish(gate_pre, up_columns)
    down_rows = rows_of(down_rows)
    up_pre = jnp.dot(normed_ffn_all, up_columns, preferred_element_type=jnp.float32)
    sigmoid_gate = jax.nn.sigmoid(gate_pre)
    silu_gate = gate_pre * sigmoid_gate
    activated_low = (silu_gate * up_pre).astype(low)
    down_part = contract_rows(activated_low, grad_ffn_all).astype(low)
    line = Line()
    down_sum = pieces_of(down_part, 2)
    line.begin(down_sum[0])
    grad_activated = times_transpose(tied(grad_ffn_all, down_part), down_rows)
    grad_gate_pre = (
        grad_activated * up_pre * sigmoid_gate * (1.0 + gate_pre * (1.0 - sigmoid_gate))
    ).astype(low)
    grad_up_pre = (grad_activated * silu_gate).astype(low)
    line.finish(grad_gate_pre, grad_up_pre)
    grad_gate_pre = line.then(grad_gate_pre)
    line.begin(*down_sum[1:2])
    grad_normed_ffn = (
        times_transpose(grad_gate_pre, gate_columns) + times_transpose(grad_up_pre, up_columns)
    ).astype(low)
    gate_part = contract_rows(normed_ffn_all, tied(grad_gate_pre, grad_normed_ffn)).astype(low)
    up_part = contract_rows(normed_ffn_all, tied(grad_up_pre, gate_part)).astype(low)
    line.finish(grad_normed_ffn, gate_part, up_part)
    grad_normed_ffn = scatter_rows(grad_normed_ffn)
    gate_sum = pieces_of(gate_part, 2)
    activated_late = line.then(activated_low)
    line.begin(gate_sum[0])
    ffn_part = jnp.dot(activated_late, down_rows, preferred_element_type=jnp.float32).astype(low)
    line.finish(ffn_part)
    up_sum = pieces_of(up_part, 2)
    grad_normed_ffn = line.then(grad_normed_ffn)
    line.begin(*gate_sum[1:])

    grad_middle_part, grad_gain_ffn = rms_backward(middle, inverse_ffn, gain_ffn, grad_normed_ffn)
    grad_middle = grad_output + grad_middle_part
    grad_branch = (RESIDUAL_SCALE * grad_middle).astype(low)
    output_part = jnp.dot(attended_low, grad_branch, preferred_element_type=jnp.float32).astype(low)
    grad_attended = times_transpose(output_all, grad_branch).astype(low)
    grad_attended, output_part = lax.optimization_barrier((grad_attended, output_part))
    output_part = scatter_low(output_part)
    line.finish(grad_attended)
    queries_again = line.then(queries)
    line.begin(up_sum[0])
    grad_query_raw, grad_key, grad_rope = attend_back(
        queries_again, key_value, rope_keys, bias, logsum, grad_attended, cosine_rows, sine_rows
    )
    line.finish(grad_query_raw)
    grad_key, grad_query_raw = line.then(grad_key), line.then(grad_query_raw)
    line.begin(*up_sum[1:])
    states = (
        (query_down, query_down_first, query_down_second),
        (query_up, query_up_first, query_up_second),
        (latent_down, latent_down_first, latent_down_second),
        (latent_up, latent_up_first, latent_up_second),
        (output_weight, output_weight_first, output_weight_second),
        (gate_weight, gate_weight_first, gate_weight_second),
        (up_weight, up_weight_first, up_weight_second),
        (down_weight, down_weight_first, down_weight_second),
        (norm_gains, norm_gains_first, norm_gains_second),
    )
    learn_rates = (
        D ** (-0.5),
        QR ** (-0.5),
        D ** (-0.5),
        KVR ** (-0.5),
        math.sqrt(sequence_length / (0.0632 * H * VD)),
        D ** (-0.5),
        D ** (-0.5),
        math.sqrt(1.0 / (0.0114 * FF)),
        0.6,
    )

    def update(slot, gradient):
        master, first_moment, second_moment = states[slot]
        return adamw_update(
            master[0],
            first_moment[0],
            second_moment[0],
            gradient.astype(jnp.float32),
            learn_rates[slot],
            0.0 if slot == 8 else WEIGHT_DECAY,
            is_owner[slot],
        )

    new_down = update(7, line.then(rows_of(down_sum)))
    key_side = jnp.concatenate([times_transpose(grad_key, latent_up_all), grad_rope[:, :ROPE]], axis=-1)
    key_side = lax.psum_scatter(
        tied(key_side.astype(low), output_part), "own", scatter_dimension=0, tiled=True
    ).astype(jnp.float32)
    latent_up_part = contract_rows(gathered_latent, grad_key).astype(low)
    query_up_part = lax.dot_general(
        query_low, grad_query_raw, (((0,), (1,)), ((), ())), preferred_element_type=jnp.float32
    ).astype(low)
    latent_up_part, query_up_part = scatter_low(latent_up_part), scatter_low(query_up_part)
    grad_query_normed = lax.dot_general(
        grad_query_raw, query_up_all, (((0,), (1,)), ((), ())), preferred_element_type=jnp.float32
    )
    grad_query_latent, grad_gain_query = rms_backward(
        query_latent, inverse_query, gain_query, grad_query_normed
    )
    line.finish(grad_query_latent, *new_down)
    output_sum = Piece(output_part)
    line.begin(output_sum)
    gate_blocks = shuffled(rows_of(gate_sum))
    line.finish()
    key_side = line.then(key_side)
    grad_key_latent, grad_gain_latent = rms_backward(
        key_latent[:, :KVR], inverse_key, gain_latent, key_side[:, :KVR]
    )
    grad_latents = jnp.concatenate(
        [grad_query_latent, grad_key_latent, unrotate(key_side[:, KVR:], cosine, sine_table)],
        axis=-1,
    ).astype(low)
    grad_normed = times_transpose(grad_latents, down_latents_all)
    grad_inputs, grad_gain_input = rms_backward(inputs, inverse_input, gain_input, grad_normed)
    input_grad = (grad_middle + grad_inputs).astype(low)
    gain_width = -(-GAINS // tokens_here)
    grad_gains = jnp.concatenate(
        [grad_gain_input, grad_gain_query, grad_gain_latent, grad_gain_ffn]
    )
    grad_gains = jnp.pad(grad_gains, (0, gain_width * tokens_here - GAINS))
    grad_latents_all = gather_rows(
        jnp.concatenate(
            [grad_latents, grad_gains.reshape(tokens_here, gain_width).astype(low)], axis=-1
        )
    )
    latent_up_sum, query_up_sum = Piece(latent_up_part), Piece(query_up_part)
    line.begin(latent_up_sum, query_up_sum)
    line.finish(gate_blocks)
    up_blocks = shuffled(rows_of(up_sum))
    gate_blocks = line.then(gate_blocks)
    ffn_branch = scatter_rows(tied(line.then(ffn_part), grad_latents_all))
    block_output = (middle + RESIDUAL_SCALE * ffn_branch).astype(low)
    latents_part = contract_rows(normed_columns, grad_latents_all[:, :width])
    grad_gains = grad_latents_all[:, width:].astype(jnp.float32)
    grad_gains = jnp.sum(grad_gains.reshape(-1, tokens_here * gain_width), axis=0)
    grad_gains = lax.dynamic_slice_in_dim(
        grad_gains, lax.axis_index("dp") * gain_count, gain_count, 0
    )
    grad_gains = jnp.pad(
        grad_gains, (0, gain_columns * query_down.shape[1] - gain_count)
    ).reshape(gain_columns, query_down.shape[1])
    latents_sum = Piece(jnp.concatenate([latents_part, grad_gains.T], axis=-1).astype(low))
    line.begin(latents_sum)
    line.finish(input_grad)
    line.begin()
    line.finish(up_blocks)
    while line.active:
        line.round()
    reduced_output, reduced_latents = output_sum.value, latents_sum.value

    reduced_latent_up, reduced_query_up = latent_up_sum.value, query_up_sum.value
    reduced_latents = reduced_latents.astype(jnp.float32)
    reduced_gains = reduced_latents[:, width:].T.reshape(-1)[:gain_count]
    reduced = (
        reduced_latents[:, :QR],
        reduced_query_up.astype(jnp.float32),
        reduced_latents[:, QR:width],
        reduced_latent_up.astype(jnp.float32),
        reduced_output.astype(jnp.float32),
        None,
        None,
        None,
        reduced_gains,
    )
    results = [block_output, input_grad]
    for slot in range(9):
        if slot in (5, 6):
            blocks = gate_blocks if slot == 5 else up_blocks
            members = (member[0] for member in states[slot])
            updated = update_joined(is_owner[slot], blocks, *members, learn_rates[slot])
        else:
            updated = new_down if slot == 7 else update(slot, reduced[slot])
        results.extend((member[None] for member in updated))
    return tuple(results)


def solution(mesh):
    return jax.shard_map(
        shards,
        mesh=mesh,
        in_specs=(
            P(("dp", "own"), None),
            P(("dp", "own"), None),
            P("dp", None),
            P(),
            P("own", "dp", None),
            P("own", "dp", None),
            P("own", "dp", None),
            P("own", "dp", None),
            P("own", "dp", None),
            P("own", "dp", None),
            P("own", "dp", None),
            P("own", "dp", None),
            P("own", "dp", None),
            P("own", "dp", None),
            P("own", "dp", None),
            P("own", "dp", None),
            P("own", "dp", None),
            P("own", "dp", None),
            P("own", "dp", None),
            P("own", "dp", None),
            P("own", "dp", None),
            P("own", "dp", None),
            P("own", "dp", None),
            P("own", "dp", None),
            P("own", "dp", None),
            P("own", "dp", None),
            P("own", "dp", None),
            P("own", "dp", None),
            P("own", "dp"),
            P("own", "dp"),
            P("own", "dp"),
        ),
        out_specs=(
            P(("dp", "own"), None),
            P(("dp", "own"), None),
            P("own", "dp", None),
            P("own", "dp", None),
            P("own", "dp", None),
            P("own", "dp", None),
            P("own", "dp", None),
            P("own", "dp", None),
            P("own", "dp", None),
            P("own", "dp", None),
            P("own", "dp", None),
            P("own", "dp", None),
            P("own", "dp", None),
            P("own", "dp", None),
            P("own", "dp", None),
            P("own", "dp", None),
            P("own", "dp", None),
            P("own", "dp", None),
            P("own", "dp", None),
            P("own", "dp", None),
            P("own", "dp", None),
            P("own", "dp", None),
            P("own", "dp", None),
            P("own", "dp", None),
            P("own", "dp", None),
            P("own", "dp", None),
            P("own", "dp"),
            P("own", "dp"),
            P("own", "dp"),
        ),
        check_vma=False,
    )
```

```python
import functools
import math

import jax
import jax.numpy as jnp
from jax import lax
from jax.experimental import pallas as pl
from jax.experimental.pallas import tpu as pltpu
from jax.sharding import PartitionSpec as P

D = 2560
H = 40
NOPE = 64
ROPE = 32
VD = 64
QR = 768
KVR = 256
FF = 6400
GAINS = 6144
HEADS_STEP = 4
LANES = 128
STEP = 7


EPSILON = 1e-05
RESIDUAL_SCALE = 1.4 / math.sqrt(62.0)
BETA_ONE = 0.5
BETA_TWO = 0.55
WEIGHT_DECAY = 0.1
ADAM_EPS = 1e-08
MASKED = -1e30
SOFTMAX_SCALE = (NOPE + ROPE) ** (-0.5)


def tied(value, *earlier):
    return lax.optimization_barrier((value, *earlier))[0]


def pieces_of(rows, most):
    for parts in range(most, 1, -1):
        if rows.shape[0] % parts == 0 and (rows.shape[0] // parts) % 8 == 0:
            return [Piece(part) for part in jnp.split(rows, parts, axis=0)]
    return [Piece(rows)]


class Piece:
    def __init__(self, value):
        self.value = value
        self.leg = 0


class Line:
    def __init__(self):
        self.count, self.place = lax.axis_size("own"), lax.axis_index("own")
        self.active = []
        self.arrived = []

    def begin(self, *new):
        self.active.extend(new)
        values = [piece.value for piece in self.active]
        if self.arrived:
            values = lax.optimization_barrier((*values, *self.arrived))
        for piece, value in zip(self.active, values):
            piece.value = value
        self.coming = [
            lax.ppermute(piece.value, "own", self.pairs(piece.leg)) for piece in self.active
        ]

    def finish(self, *inside):
        last, half = self.count - 1, self.count // 2
        self.arrived = list(lax.optimization_barrier(tuple(self.coming)))
        for piece, arrived in zip(self.active, self.arrived):
            value = tied(piece.value, *inside) if inside else piece.value
            if piece.leg < half:
                piece.value = value + arrived
            else:
                outer = last - 1 - piece.leg
                ended = (self.place == outer) | (self.place == last - outer)
                piece.value = jnp.where(ended, arrived, value)
            piece.leg += 1
        self.active = [piece for piece in self.active if piece.leg < last]

    def round(self, *new):
        self.begin(*new)
        self.finish()

    def pairs(self, leg):
        last, half = self.count - 1, self.count // 2
        if leg == half - 1:
            return [(half - 1, half), (half, half - 1)]
        near, far = (leg, leg + 1) if leg < half else (last - leg, last - 1 - leg)
        return [(near, far), (last - near, last - far)]

    def then(self, value):
        return tied(value, *self.arrived)


def shuffled(columns):
    shares = lax.axis_size("dp")
    blocks = columns.reshape(shares, columns.shape[0] // shares, columns.shape[1])
    return lax.all_to_all(blocks, "dp", 0, 0)


def update_kernel(
    learn_rate,
    weight_decay,
    owner_ref,
    blocks_ref,
    master_ref,
    first_ref,
    second_ref,
    new_master_ref,
    new_first_ref,
    new_second_ref,
    gradient_ref,
):
    @pl.when(owner_ref[0] == 1)
    def _():
        width = blocks_ref.shape[2]
        for number in range(blocks_ref.shape[0]):
            gradient_ref[:, number * width : (number + 1) * width] = blocks_ref[number].astype(
                jnp.float32
            )
        gradient, master = gradient_ref[...], master_ref[...]
        new_first = BETA_ONE * first_ref[...] + (1.0 - BETA_ONE) * gradient
        new_second = BETA_TWO * second_ref[...] + (1.0 - BETA_TWO) * gradient * gradient
        mean_hat = new_first / (1.0 - BETA_ONE**STEP)
        square_hat = new_second / (1.0 - BETA_TWO**STEP)
        new_master_ref[...] = master - learn_rate * (
            mean_hat / (jnp.sqrt(square_hat) + ADAM_EPS) + weight_decay * master
        )
        new_first_ref[...] = new_first
        new_second_ref[...] = new_second

    @pl.when(owner_ref[0] != 1)
    def _():
        new_master_ref[...] = master_ref[...]
        new_first_ref[...] = first_ref[...]
        new_second_ref[...] = second_ref[...]


def update_joined(is_owner, blocks, master, first_moment, second_moment, learn_rate):
    rows, columns = master.shape
    step_rows = next(size for size in (64, 32, 16, rows) if rows % size == 0)
    state = pl.BlockSpec((step_rows, columns), lambda i, _: (i, 0))
    return pl.pallas_call(
        functools.partial(update_kernel, learn_rate, WEIGHT_DECAY),
        grid_spec=pltpu.PrefetchScalarGridSpec(
            num_scalar_prefetch=1,
            grid=(rows // step_rows,),
            in_specs=[
                pl.BlockSpec((blocks.shape[0], step_rows, blocks.shape[2]), lambda i, _: (0, i, 0)),
                state,
                state,
                state,
            ],
            out_specs=[state, state, state],
            scratch_shapes=[pltpu.VMEM((step_rows, columns), jnp.float32)],
        ),
        out_shape=[jax.ShapeDtypeStruct(master.shape, jnp.float32)] * 3,
        cost_estimate=pl.CostEstimate(
            flops=20 * rows * columns, bytes_accessed=26 * rows * columns, transcendentals=0
        ),
        compiler_params=pltpu.CompilerParams(vmem_limit_bytes=48 * 1024 * 1024),
    )(is_owner.astype(jnp.int32).reshape(1), blocks, master, first_moment, second_moment)


def rows_of(pieces):
    return jnp.concatenate([piece.value for piece in pieces], axis=0)


def gather_rows(rows):
    return lax.all_gather(rows, "dp", axis=0, tiled=True)


def scatter_low(rows):
    return lax.psum_scatter(rows, "dp", scatter_dimension=0, tiled=True)


def scatter_rows(rows):
    return scatter_low(rows).astype(jnp.float32)


def rms_forward(values, norm_gain):
    inverse = lax.rsqrt(jnp.mean(values * values, axis=-1, keepdims=True) + EPSILON)
    return (values * inverse * norm_gain, inverse)


def rms_backward(values, inverse, norm_gain, grad_normed):
    normed = values * inverse
    grad_gain = jnp.sum(grad_normed * normed, axis=0)
    scaled = grad_normed * norm_gain
    grad_values = inverse * (scaled - normed * jnp.mean(scaled * normed, axis=-1, keepdims=True))
    return (grad_values, grad_gain)


def rotary_tables(positions):
    half_width = ROPE // 2
    frequency = 10000.0 ** (-jnp.arange(half_width, dtype=jnp.float32) / half_width)
    angles = positions.astype(jnp.float32)[:, None] * frequency[None, :]
    return (jnp.cos(angles), jnp.sin(angles))


def rotate(values, cosine, sine_table):
    half_width = values.shape[-1] // 2
    former = values[..., :half_width]
    latter = values[..., half_width:]
    return jnp.concatenate(
        [former * cosine - latter * sine_table, latter * cosine + former * sine_table], axis=-1
    )


def unrotate(gradient, cosine, sine_table):
    half_width = gradient.shape[-1] // 2
    former = gradient[..., :half_width]
    latter = gradient[..., half_width:]
    return jnp.concatenate(
        [former * cosine + latter * sine_table, latter * cosine - former * sine_table], axis=-1
    )


def contract_rows(first_matrix, second_matrix):
    return lax.dot_general(
        first_matrix, second_matrix, (((0,), (0,)), ((), ())), preferred_element_type=jnp.float32
    )


def times_transpose(first_matrix, second_matrix):
    return lax.dot_general(
        first_matrix, second_matrix, (((1,), (1,)), ((), ())), preferred_element_type=jnp.float32
    )


def wide_query(query):
    tokens=query.shape[1]
    zero=lambda rows: jnp.zeros((rows,tokens),query.dtype)
    return jnp.concatenate([query[:NOPE],zero(VD),query[NOPE:],zero(128-ROPE)],axis=0)

def attend_kernel(query_ref,kv_ref,rope_ref,bias_ref,out_ref,log_ref):
    rope=rope_ref[...]
    for head in range(HEADS_STEP):
        query=wide_query(query_ref[head*(NOPE+ROPE):(head+1)*(NOPE+ROPE),:])
        kv=kv_ref[:,head*(NOPE+VD):(head+1)*(NOPE+VD)]
        keys=jnp.concatenate([kv,rope],axis=1)
        scores=jnp.dot(keys,query,preferred_element_type=jnp.float32) * SOFTMAX_SCALE+bias_ref[...]
        peak=jnp.max(scores,axis=0,keepdims=True)
        exponent=jnp.exp(scores-peak)
        total=jnp.sum(exponent,axis=0,keepdims=True)
        weights=(exponent*(1.0/total)).astype(jnp.bfloat16)
        out=contract_rows(kv,weights)
        out_ref[head*VD:(head+1)*VD,:]=out[NOPE:].astype(out_ref.dtype)
        log_ref[head]=peak+jnp.log(total)

def attend(query,kv,rope,bias,first,heads):
    tokens=query.shape[1]; length=kv.shape[0]
    return pl.pallas_call(
        attend_kernel,
        grid=(heads//HEADS_STEP,),
        in_specs=[
            pl.BlockSpec((HEADS_STEP*(NOPE+ROPE),tokens),lambda i:(i+first//HEADS_STEP,0)),
            pl.BlockSpec((length,HEADS_STEP*(NOPE+VD)),lambda i:(0,i+first//HEADS_STEP)),
            pl.BlockSpec((length,128),lambda i:(0,0)),
            pl.BlockSpec((length,tokens),lambda i:(0,0)),
        ],
        out_specs=[
            pl.BlockSpec((HEADS_STEP*VD,tokens),lambda i:(i,0)),
            pl.BlockSpec((HEADS_STEP,1,tokens),lambda i:(i,0,0)),
        ],
        out_shape=[jax.ShapeDtypeStruct((heads*VD,tokens),jnp.bfloat16),jax.ShapeDtypeStruct((heads,1,tokens),jnp.float32)],
        compiler_params=pltpu.CompilerParams(vmem_limit_bytes=48*1024*1024),
    )(query,kv,rope,bias)

def attend_back_kernel(query_ref,kv_ref,rope_ref,bias_ref,log_ref,grad_ref,cos_ref,sin_ref,dq_ref,dkv_ref,dr_ref):
    rope=rope_ref[...]
    half=ROPE//2
    @pl.when(pl.program_id(0)==0)
    def _():
        dr_ref[...]=jnp.zeros_like(dr_ref)
    for head in range(HEADS_STEP):
        query=wide_query(query_ref[head*(NOPE+ROPE):(head+1)*(NOPE+ROPE),:])
        kv=kv_ref[:,head*(NOPE+VD):(head+1)*(NOPE+VD)]
        grad=grad_ref[head*VD:(head+1)*VD,:]
        grad=jnp.concatenate([jnp.zeros((NOPE,grad.shape[1]),grad.dtype),grad],axis=0)
        keys=jnp.concatenate([kv,rope],axis=1)
        scores=jnp.dot(keys,query,preferred_element_type=jnp.float32) * SOFTMAX_SCALE+bias_ref[...]
        weights=jnp.exp(scores-log_ref[head])
        grad_weights=jnp.dot(kv,grad,preferred_element_type=jnp.float32)
        inner=jnp.sum(weights*grad_weights,axis=0,keepdims=True)
        grad_scores=(weights*(grad_weights-inner)).astype(jnp.bfloat16)
        key_side=times_transpose(grad_scores,query) * SOFTMAX_SCALE
        dkv=key_side[:,:128]+times_transpose(weights.astype(jnp.bfloat16),grad)
        dkv_ref[:,head*(NOPE+VD):(head+1)*(NOPE+VD)]=dkv.astype(dkv_ref.dtype)
        dr_ref[...]+=key_side[:,128:]
        dq=contract_rows(keys,grad_scores) * SOFTMAX_SCALE
        former=dq[128:128+half]; latter=dq[128+half:128+ROPE]
        base=head*(NOPE+ROPE)
        dq_ref[base:base+NOPE,:]=dq[:NOPE].astype(dq_ref.dtype)
        dq_ref[base+NOPE:base+NOPE+half,:]=(former*cos_ref[...]+latter*sin_ref[...]).astype(dq_ref.dtype)
        dq_ref[base+NOPE+half:base+NOPE+ROPE,:]=(latter*cos_ref[...]-former*sin_ref[...]).astype(dq_ref.dtype)

def attend_back(query,kv,rope,bias,logs,grad,cos,sin):
    tokens=query.shape[1]; length=kv.shape[0]
    return pl.pallas_call(
        attend_back_kernel,
        grid=(H//HEADS_STEP,),
        in_specs=[
            pl.BlockSpec((HEADS_STEP*(NOPE+ROPE),tokens),lambda i:(i,0)),
            pl.BlockSpec((length,HEADS_STEP*(NOPE+VD)),lambda i:(0,i)),
            pl.BlockSpec((length,128),lambda i:(0,0)),
            pl.BlockSpec((length,tokens),lambda i:(0,0)),
            pl.BlockSpec((HEADS_STEP,1,tokens),lambda i:(i,0,0)),
            pl.BlockSpec((HEADS_STEP*VD,tokens),lambda i:(i,0)),
            pl.BlockSpec((ROPE//2,tokens),lambda i:(0,0)),
            pl.BlockSpec((ROPE//2,tokens),lambda i:(0,0)),
        ],
        out_specs=[
            pl.BlockSpec((HEADS_STEP*(NOPE+ROPE),tokens),lambda i:(i,0)),
            pl.BlockSpec((length,HEADS_STEP*(NOPE+VD)),lambda i:(0,i)),
            pl.BlockSpec((length,128),lambda i:(0,0)),
        ],
        out_shape=[jax.ShapeDtypeStruct((H*(NOPE+ROPE),tokens),jnp.bfloat16),
                   jax.ShapeDtypeStruct((length,H*(NOPE+VD)),jnp.bfloat16),
                   jax.ShapeDtypeStruct((length,128),jnp.float32)],
        compiler_params=pltpu.CompilerParams(vmem_limit_bytes=48*1024*1024),
    )(query,kv,rope,bias,logs,grad,cos,sin)


def adamw_update(master, first_moment, second_moment, gradient, learn_rate, weight_decay, is_owner):
    new_first = BETA_ONE * first_moment + (1.0 - BETA_ONE) * gradient
    new_second = BETA_TWO * second_moment + (1.0 - BETA_TWO) * gradient * gradient
    mean_hat = new_first / (1.0 - BETA_ONE**STEP)
    square_hat = new_second / (1.0 - BETA_TWO**STEP)
    new_master = master - learn_rate * (
        mean_hat / (jnp.sqrt(square_hat) + ADAM_EPS) + weight_decay * master
    )
    return (
        jnp.where(is_owner, new_master, master),
        jnp.where(is_owner, new_first, first_moment),
        jnp.where(is_owner, new_second, second_moment),
    )


def shards(
    hidden,
    cotangent,
    block_index,
    owners,
    query_down,
    query_down_first,
    query_down_second,
    query_up,
    query_up_first,
    query_up_second,
    latent_down,
    latent_down_first,
    latent_down_second,
    latent_up,
    latent_up_first,
    latent_up_second,
    output_weight,
    output_weight_first,
    output_weight_second,
    gate_weight,
    gate_weight_first,
    gate_weight_second,
    up_weight,
    up_weight_first,
    up_weight_second,
    down_weight,
    down_weight_first,
    down_weight_second,
    norm_gains,
    norm_gains_first,
    norm_gains_second,
):
    own_count = lax.axis_size("own")
    own_place = lax.axis_index("own")
    tokens_here = hidden.shape[0]
    sequence_length = tokens_here * own_count
    low = jnp.bfloat16
    inputs = hidden.astype(jnp.float32)
    is_owner = [own_place == owners[slot] for slot in range(9)]
    def owned(slot, tensor):
        return jnp.where(is_owner[slot], tensor[0], 0.0).astype(low)

    gain_count = norm_gains.shape[1]
    gain_columns = -(-gain_count // query_down.shape[1])
    gain_block = jnp.pad(
        owned(8, norm_gains), (0, gain_columns * query_down.shape[1] - gain_count)
    ).reshape(gain_columns, query_down.shape[1])
    width = QR + KVR + ROPE
    line = Line()
    down_latents = Piece(
        jnp.concatenate([owned(0, query_down), owned(2, latent_down), gain_block.T], axis=-1)
    )
    query_up_rows = Piece(owned(1, query_up))
    latent_up_rows = Piece(owned(3, latent_up))
    output_rows = Piece(owned(4, output_weight))
    gate_rows = pieces_of(owned(5, gate_weight), 2)
    up_rows = pieces_of(owned(6, up_weight), 2)
    down_rows = pieces_of(owned(7, down_weight), 2)
    grad_ffn_all = gather_rows(
        (RESIDUAL_SCALE * cotangent.astype(jnp.float32)).astype(low)
    )
    line.round(down_latents)
    line.begin(query_up_rows, latent_up_rows)
    line.finish(output_rows.value, *[piece.value for piece in gate_rows])
    line.begin(output_rows)
    line.finish(*[piece.value for piece in up_rows + down_rows])
    down_latents_all = gather_rows(tied(down_latents.value, grad_ffn_all))
    line.round(gate_rows[0])
    query_up_all = gather_rows(query_up_rows.value)
    latent_up_all = gather_rows(latent_up_rows.value)
    down_latents_all = line.then(down_latents_all)
    gains_float = down_latents_all[:, width:].reshape(-1, query_down.shape[1], gain_columns)
    gains_float = gains_float.transpose(0, 2, 1).reshape(-1, gain_columns * query_down.shape[1])
    gains_float = gains_float[:, :gain_count].reshape(-1).astype(jnp.float32)
    down_latents_all = down_latents_all[:, :width]
    gain_input = gains_float[:D]
    gain_query = gains_float[D : D + QR]
    gain_latent = gains_float[D + QR : D + QR + KVR]
    gain_ffn = gains_float[D + QR + KVR :]

    grad_output = cotangent.astype(jnp.float32)

    normed, inverse_input = rms_forward(inputs, gain_input)
    normed_low = normed.astype(low)
    latents = jnp.dot(normed_low, down_latents_all, preferred_element_type=jnp.float32)
    query_latent = latents[:, :QR]
    key_latent = latents[:, QR:]
    query_normed, inverse_query = rms_forward(query_latent, gain_query)
    query_low = query_normed.astype(low)
    positions = own_place * tokens_here + jnp.arange(tokens_here, dtype=jnp.int32)
    cosine, sine_table = rotary_tables(positions)
    key_normed, inverse_key = rms_forward(key_latent[:, :KVR], gain_latent)
    key_low = key_normed.astype(low)
    rope_low = rotate(key_latent[:, KVR:], cosine, sine_table).astype(low)
    gathered_keys = lax.all_gather(
        jnp.concatenate([key_low, rope_low], axis=-1), "own", axis=0, tiled=True
    )
    gate_rows[-1].value = tied(gate_rows[-1].value, gathered_keys)
    line.begin(*gate_rows[1:])
    gathered_latent = gathered_keys[:, :KVR]
    rope_keys = jnp.pad(gathered_keys[:, KVR:], ((0, 0), (0, LANES - ROPE)))
    query_raw = lax.dot_general(
        query_up_all, query_low, (((0,), (1,)), ((), ())), preferred_element_type=jnp.float32
    ).reshape(H, NOPE + ROPE, tokens_here)
    cosine_rows, sine_rows = cosine.T, sine_table.T
    former, latter = jnp.split(query_raw[:, NOPE:], 2, axis=1)
    queries = jnp.concatenate(
        [
            query_raw[:, :NOPE],
            former * cosine_rows - latter * sine_rows,
            latter * cosine_rows + former * sine_rows,
        ],
        axis=1,
    )
    queries = queries.astype(low).reshape(H * (NOPE + ROPE), tokens_here)
    key_value = jnp.dot(gathered_latent, latent_up_all, preferred_element_type=jnp.float32).astype(
        low
    )
    line.finish(key_value)
    output_all = gather_rows(output_rows.value)
    sequence_blocks = block_index[0]
    query_blocks = lax.dynamic_slice_in_dim(
        sequence_blocks, own_place * tokens_here, tokens_here, 0
    )
    bias = jnp.where(sequence_blocks[:, None] <= query_blocks[None, :], 0.0, MASKED)
    bias = bias.astype(jnp.float32)
    half_heads = H // 2
    line.begin(up_rows[0])
    attended_first, logsum_first = attend(
        queries, line.then(key_value), rope_keys, bias, 0, half_heads
    )
    line.finish(attended_first)
    queries_second = line.then(queries)
    line.begin(*up_rows[1:])
    attended_second, logsum_second = attend(
        queries_second, key_value, rope_keys, bias, half_heads, H - half_heads
    )
    line.finish(attended_second)
    attended_low = line.then(jnp.concatenate([attended_first, attended_second], axis=0))
    logsum = jnp.concatenate([logsum_first, logsum_second], axis=0)
    line.begin(down_rows[0])
    branch = contract_rows(attended_low, output_all)
    middle = inputs + RESIDUAL_SCALE * branch
    normed_ffn, inverse_ffn = rms_forward(middle, gain_ffn)

    normed_ffn_low = normed_ffn.astype(low)
    line.finish(normed_ffn_low)
    normed_ffn_all = gather_rows(normed_ffn_low)
    normed_columns = lax.all_to_all(line.then(normed_low), "dp", 1, 0, tiled=True)
    gate_rows = line.then(rows_of(gate_rows))
    line.begin(*down_rows[1:])
    gate_columns = lax.all_to_all(gate_rows, "dp", 1, 0, tiled=True)
    line.finish()
    line.begin()
    up_columns = lax.all_to_all(line.then(rows_of(up_rows)), "dp", 1, 0, tiled=True)
    line.finish(normed_ffn_all, gate_columns, normed_columns)
    line.begin()
    gate_pre = jnp.dot(
        line.then(normed_ffn_all), gate_columns, preferred_element_type=jnp.float32
    )
    line.finish(gate_pre, up_columns)
    down_rows = rows_of(down_rows)
    up_pre = jnp.dot(normed_ffn_all, up_columns, preferred_element_type=jnp.float32)
    sigmoid_gate = jax.nn.sigmoid(gate_pre)
    silu_gate = gate_pre * sigmoid_gate
    activated_low = (silu_gate * up_pre).astype(low)
    down_part = contract_rows(activated_low, grad_ffn_all).astype(low)
    line = Line()
    down_sum = pieces_of(down_part, 2)
    line.begin(down_sum[0])
    grad_activated = times_transpose(tied(grad_ffn_all, down_part), down_rows)
    grad_gate_pre = (
        grad_activated * up_pre * sigmoid_gate * (1.0 + gate_pre * (1.0 - sigmoid_gate))
    ).astype(low)
    grad_up_pre = (grad_activated * silu_gate).astype(low)
    line.finish(grad_gate_pre, grad_up_pre)
    grad_gate_pre = line.then(grad_gate_pre)
    line.begin(*down_sum[1:2])
    grad_normed_ffn = (
        times_transpose(grad_gate_pre, gate_columns) + times_transpose(grad_up_pre, up_columns)
    ).astype(low)
    gate_part = contract_rows(normed_ffn_all, tied(grad_gate_pre, grad_normed_ffn)).astype(low)
    up_part = contract_rows(normed_ffn_all, tied(grad_up_pre, gate_part)).astype(low)
    line.finish(grad_normed_ffn, gate_part, up_part)
    grad_normed_ffn = scatter_rows(grad_normed_ffn)
    gate_sum = pieces_of(gate_part, 2)
    activated_late = line.then(activated_low)
    line.begin(gate_sum[0])
    ffn_part = jnp.dot(activated_late, down_rows, preferred_element_type=jnp.float32).astype(low)
    line.finish(ffn_part)
    up_sum = pieces_of(up_part, 2)
    grad_normed_ffn = line.then(grad_normed_ffn)
    line.begin(*gate_sum[1:])

    grad_middle_part, grad_gain_ffn = rms_backward(middle, inverse_ffn, gain_ffn, grad_normed_ffn)
    grad_middle = grad_output + grad_middle_part
    grad_branch = (RESIDUAL_SCALE * grad_middle).astype(low)
    output_part = jnp.dot(attended_low, grad_branch, preferred_element_type=jnp.float32).astype(low)
    grad_attended = times_transpose(output_all, grad_branch).astype(low)
    grad_attended, output_part = lax.optimization_barrier((grad_attended, output_part))
    output_part = scatter_low(output_part)
    line.finish(grad_attended)
    queries_again = line.then(queries)
    line.begin(up_sum[0])
    grad_query_raw, grad_key, grad_rope = attend_back(
        queries_again, key_value, rope_keys, bias, logsum, grad_attended, cosine_rows, sine_rows
    )
    line.finish(grad_query_raw)
    grad_key, grad_query_raw = line.then(grad_key), line.then(grad_query_raw)
    line.begin(*up_sum[1:])
    states = (
        (query_down, query_down_first, query_down_second),
        (query_up, query_up_first, query_up_second),
        (latent_down, latent_down_first, latent_down_second),
        (latent_up, latent_up_first, latent_up_second),
        (output_weight, output_weight_first, output_weight_second),
        (gate_weight, gate_weight_first, gate_weight_second),
        (up_weight, up_weight_first, up_weight_second),
        (down_weight, down_weight_first, down_weight_second),
        (norm_gains, norm_gains_first, norm_gains_second),
    )
    learn_rates = (
        D ** (-0.5),
        QR ** (-0.5),
        D ** (-0.5),
        KVR ** (-0.5),
        math.sqrt(sequence_length / (0.0632 * H * VD)),
        D ** (-0.5),
        D ** (-0.5),
        math.sqrt(1.0 / (0.0114 * FF)),
        0.6,
    )

    def update(slot, gradient):
        master, first_moment, second_moment = states[slot]
        return adamw_update(
            master[0],
            first_moment[0],
            second_moment[0],
            gradient.astype(jnp.float32),
            learn_rates[slot],
            0.0 if slot == 8 else WEIGHT_DECAY,
            is_owner[slot],
        )

    new_down = update(7, line.then(rows_of(down_sum)))
    key_side = jnp.concatenate([times_transpose(grad_key, latent_up_all), grad_rope[:, :ROPE]], axis=-1)
    key_side = lax.psum_scatter(
        tied(key_side.astype(low), output_part), "own", scatter_dimension=0, tiled=True
    ).astype(jnp.float32)
    latent_up_part = contract_rows(gathered_latent, grad_key).astype(low)
    query_up_part = lax.dot_general(
        query_low, grad_query_raw, (((0,), (1,)), ((), ())), preferred_element_type=jnp.float32
    ).astype(low)
    latent_up_part, query_up_part = scatter_low(latent_up_part), scatter_low(query_up_part)
    grad_query_normed = lax.dot_general(
        grad_query_raw, query_up_all, (((0,), (1,)), ((), ())), preferred_element_type=jnp.float32
    )
    grad_query_latent, grad_gain_query = rms_backward(
        query_latent, inverse_query, gain_query, grad_query_normed
    )
    line.finish(grad_query_latent, *new_down)
    output_sum = Piece(output_part)
    line.begin(output_sum)
    gate_blocks = shuffled(rows_of(gate_sum))
    line.finish()
    key_side = line.then(key_side)
    grad_key_latent, grad_gain_latent = rms_backward(
        key_latent[:, :KVR], inverse_key, gain_latent, key_side[:, :KVR]
    )
    grad_latents = jnp.concatenate(
        [grad_query_latent, grad_key_latent, unrotate(key_side[:, KVR:], cosine, sine_table)],
        axis=-1,
    ).astype(low)
    grad_normed = times_transpose(grad_latents, down_latents_all)
    grad_inputs, grad_gain_input = rms_backward(inputs, inverse_input, gain_input, grad_normed)
    input_grad = (grad_middle + grad_inputs).astype(low)
    gain_width = -(-GAINS // tokens_here)
    grad_gains = jnp.concatenate(
        [grad_gain_input, grad_gain_query, grad_gain_latent, grad_gain_ffn]
    )
    grad_gains = jnp.pad(grad_gains, (0, gain_width * tokens_here - GAINS))
    grad_latents_all = gather_rows(
        jnp.concatenate(
            [grad_latents, grad_gains.reshape(tokens_here, gain_width).astype(low)], axis=-1
        )
    )
    latent_up_sum, query_up_sum = Piece(latent_up_part), Piece(query_up_part)
    line.begin(latent_up_sum, query_up_sum)
    line.finish(gate_blocks)
    up_blocks = shuffled(rows_of(up_sum))
    gate_blocks = line.then(gate_blocks)
    ffn_branch = scatter_rows(tied(line.then(ffn_part), grad_latents_all))
    block_output = (middle + RESIDUAL_SCALE * ffn_branch).astype(low)
    latents_part = contract_rows(normed_columns, grad_latents_all[:, :width])
    grad_gains = grad_latents_all[:, width:].astype(jnp.float32)
    grad_gains = jnp.sum(grad_gains.reshape(-1, tokens_here * gain_width), axis=0)
    grad_gains = lax.dynamic_slice_in_dim(
        grad_gains, lax.axis_index("dp") * gain_count, gain_count, 0
    )
    grad_gains = jnp.pad(
        grad_gains, (0, gain_columns * query_down.shape[1] - gain_count)
    ).reshape(gain_columns, query_down.shape[1])
    latents_sum = Piece(jnp.concatenate([latents_part, grad_gains.T], axis=-1).astype(low))
    line.begin(latents_sum)
    line.finish(input_grad)
    line.begin()
    line.finish()
    line.begin()
    line.finish(up_blocks)
    while line.active:
        line.round()
    reduced_output, reduced_latents = output_sum.value, latents_sum.value

    reduced_latent_up, reduced_query_up = latent_up_sum.value, query_up_sum.value
    reduced_latents = reduced_latents.astype(jnp.float32)
    reduced_gains = reduced_latents[:, width:].T.reshape(-1)[:gain_count]
    reduced = (
        reduced_latents[:, :QR],
        reduced_query_up.astype(jnp.float32),
        reduced_latents[:, QR:width],
        reduced_latent_up.astype(jnp.float32),
        reduced_output.astype(jnp.float32),
        None,
        None,
        None,
        reduced_gains,
    )
    results = [block_output, input_grad]
    for slot in range(9):
        if slot in (5, 6):
            blocks = gate_blocks if slot == 5 else up_blocks
            members = (member[0] for member in states[slot])
            updated = update_joined(is_owner[slot], blocks, *members, learn_rates[slot])
        else:
            updated = new_down if slot == 7 else update(slot, reduced[slot])
        results.extend((member[None] for member in updated))
    return tuple(results)


def solution(mesh):
    return jax.shard_map(
        shards,
        mesh=mesh,
        in_specs=(
            P(("dp", "own"), None),
            P(("dp", "own"), None),
            P("dp", None),
            P(),
            P("own", "dp", None),
            P("own", "dp", None),
            P("own", "dp", None),
            P("own", "dp", None),
            P("own", "dp", None),
            P("own", "dp", None),
            P("own", "dp", None),
            P("own", "dp", None),
            P("own", "dp", None),
            P("own", "dp", None),
            P("own", "dp", None),
            P("own", "dp", None),
            P("own", "dp", None),
            P("own", "dp", None),
            P("own", "dp", None),
            P("own", "dp", None),
            P("own", "dp", None),
            P("own", "dp", None),
            P("own", "dp", None),
            P("own", "dp", None),
            P("own", "dp", None),
            P("own", "dp", None),
            P("own", "dp", None),
            P("own", "dp", None),
            P("own", "dp"),
            P("own", "dp"),
            P("own", "dp"),
        ),
        out_specs=(
            P(("dp", "own"), None),
            P(("dp", "own"), None),
            P("own", "dp", None),
            P("own", "dp", None),
            P("own", "dp", None),
            P("own", "dp", None),
            P("own", "dp", None),
            P("own", "dp", None),
            P("own", "dp", None),
            P("own", "dp", None),
            P("own", "dp", None),
            P("own", "dp", None),
            P("own", "dp", None),
            P("own", "dp", None),
            P("own", "dp", None),
            P("own", "dp", None),
            P("own", "dp", None),
            P("own", "dp", None),
            P("own", "dp", None),
            P("own", "dp", None),
            P("own", "dp", None),
            P("own", "dp", None),
            P("own", "dp", None),
            P("own", "dp", None),
            P("own", "dp", None),
            P("own", "dp", None),
            P("own", "dp"),
            P("own", "dp"),
            P("own", "dp"),
        ),
        check_vma=False,
    )
```
